512 devices in a mesh: dp: 32 (over y_hi, x, core), seq: 16 (over z, y_lo).
Axes of the slice: x: 4, y: 8 (y_hi: 4, y_lo: 2; y = y_hi * 2 + y_lo), z: 8, core: 2. Of those that a mesh axis runs over, the one named last changes fastest.
Arguments:
- query_rows: bfloat16 [32, 2048, 2048], P('dp', 'seq'), may hold values from -108 to 108
- key_rows: bfloat16 [32, 2048, 2048], P('dp', 'seq'), may hold values from -6 to 6
- value_rows: bfloat16 [32, 2048, 2048], P('dp', 'seq'), may hold values from -6 to 6
- out_weight: bfloat16 [2048, 2048], P('seq', 'dp'), may hold values from -0.125 to 0.125
- grad_out: bfloat16 [32, 2048, 2048], P('dp', 'seq'), may hold values from -6 to 6
- block_list: int32 [32, 32, 8], P('dp'), may hold values from 0 to 31, as said below
Outputs:
- attended: bfloat16 [32, 2048, 2048], P('dp', 'seq')
- query_gradient: bfloat16 [32, 2048, 2048], P('dp', 'seq')
- grad_key: bfloat16 [32, 2048, 2048], P('dp', 'seq')
- grad_value: bfloat16 [32, 2048, 2048], P('dp', 'seq')
- grad_weight: float32 [2048, 2048], P('seq', 'dp')
The draws below stay inside these ranges and needn't reach their ends.
Inputs may be any that keep to these rules, and one draw needn't show every extreme that they name: `block_list`: for query block b, slots 0 to 2 hold b - 1, b, b + 1 modulo 32, slots 3 and 4 hold 0 and 31, slots 5 to 7 are drawn at random; the same list serves all heads.
All inputs are finite; a program needn't handle non-finite values.
Results may differ from the reference program's by a relative error of at most 0.0075.
Values may be sent and summed in bfloat16 or wider, within the bound.
A program may use at most 128 MiB of HBM per device.

```python
import math
import jax
import jax.numpy as jnp
from jax import lax

HEADS = 16
HEAD_SIZE = 128
BLOCK = 64
SLOTS = 8
D = 2048
SEQUENCE_LENGTH = 2048
SEQUENCES = 32


def paired_draw(key):
    base_key = jax.random.fold_in(key, 11)
    first, second = jax.random.split(base_key, 2)
    shape = (SEQUENCES, SEQUENCE_LENGTH, D)
    queries = jnp.clip(jax.random.normal(first, shape, jnp.float32), -6.0, 6.0)
    keyed = jnp.clip(jax.random.normal(second, shape, jnp.float32), -6.0, 6.0)
    return (queries, keyed)


def draw_query_rows(key, part):
    return paired_draw(key)[0].astype(jnp.bfloat16)


def draw_key_rows(key, part):
    return paired_draw(key)[1].astype(jnp.bfloat16)


def draw_block_list(key, part):
    block_count = SEQUENCE_LENGTH // BLOCK
    block_ids = jnp.arange(block_count, dtype=jnp.int32)
    window = jnp.stack([(block_ids - 1) % block_count, block_ids, (block_ids + 1) % block_count], axis=-1)
    edges = jnp.stack([jnp.zeros_like(block_ids), jnp.full_like(block_ids, block_count - 1)], axis=-1)
    fixed_part = jnp.concatenate([window, edges], axis=-1)
    fixed_part = jnp.broadcast_to(fixed_part[None], (SEQUENCES, block_count, 5))
    random_ids = jax.random.randint(jax.random.fold_in(key, 7), (SEQUENCES, block_count, 3), 0, block_count, dtype=jnp.int32)
    return jnp.concatenate([fixed_part, random_ids], axis=-1).astype(jnp.int32)


def raised(entries, rng, source, target, blocks, factor):
    def block_of(dim):
        return (jnp.arange(entries.shape[dim]) // (entries.shape[dim] // blocks)).reshape((-1,) + (1,) * (entries.ndim - 1 - dim))

    one_side = jax.random.permutation(rng, blocks)[block_of(target)]
    other_side = (block_of(target) + blocks // 2) % blocks
    return jnp.where((block_of(source) == one_side) | (block_of(source) == other_side), factor * entries, entries)


def block_levels(own_key, shape, cuts, smallest, high):
    def one(axis_at, shards_of):
        heights = jax.random.uniform(jax.random.fold_in(jax.random.fold_in(own_key, 6), axis_at), (shards_of,), jnp.float32, smallest / len(cuts), high / len(cuts))
        return jnp.repeat(jnp.exp(heights), shape[axis_at] // shards_of).reshape((-1,) + (1,) * (len(shape) - axis_at - 1))

    level = one(*cuts[0])
    for cut in cuts[1:]:
        level = level * one(*cut)
    return level


def scatter_about(key, extent, deviation, most, shards=(), kind=jnp.bfloat16):
    drawn = jax.random.normal(key, extent, jnp.float32) * deviation
    if len(shards) > 0:
        drawn = block_levels(key, extent, shards, -0.22, 0.18) * drawn
    return jnp.clip(drawn, min=-most, max=most).astype(kind)


def bell_draw_with(stream_key, shape, width, bound, pieces, heavy, held_as=jnp.bfloat16):
    result = width * jax.random.normal(stream_key, shape, jnp.float32)
    if pieces:
        result = result * block_levels(stream_key, shape, pieces, -0.22, 0.18)
    return jnp.clip(raised(result, jax.random.fold_in(stream_key, 3), *heavy), -bound, bound).astype(held_as)


def setup_inputs(seed: int = 0) -> dict:
    keys = jax.random.split(jax.random.key(seed), 7)
    query_rows = draw_query_rows(jax.random.fold_in(keys[6], 71), 0)
    key_rows = draw_key_rows(jax.random.fold_in(keys[6], 71), 0)
    value_rows = scatter_about(keys[2], (SEQUENCES, SEQUENCE_LENGTH, D), 1.0, 6.0, ((0, 32), (1, 16)))
    out_weight = scatter_about(keys[3], (D, D), D ** -0.5, 0.125, ((0, 16), (1, 32)))
    grad_out = bell_draw_with(keys[4], (SEQUENCES, SEQUENCE_LENGTH, D), 1.0, 6.0, ((0, 32), (1, 16)), (0, 2, 32, 2.75))
    block_list = draw_block_list(jax.random.fold_in(keys[6], 71), 0)
    return dict(query_rows=query_rows, key_rows=key_rows, value_rows=value_rows, out_weight=out_weight, grad_out=grad_out, block_list=block_list)


def rounded(values):
    return lax.optimization_barrier(values.astype(jnp.bfloat16)).astype(jnp.float32)

def head_pass(query_head, key_head, value_head, grad_head, block_ids):
    block_count = SEQUENCE_LENGTH // BLOCK
    logit_scale = 1.0 / math.sqrt(HEAD_SIZE)
    blocked_queries = query_head.astype(jnp.float32).reshape(block_count, BLOCK, HEAD_SIZE)
    key_block_indices = key_head.astype(jnp.float32).reshape(block_count, BLOCK, HEAD_SIZE)[block_ids]
    key_block_indices = key_block_indices.reshape(block_count, SLOTS * BLOCK, HEAD_SIZE)
    value_block_indices = value_head.astype(jnp.float32).reshape(block_count, BLOCK, HEAD_SIZE)[block_ids]
    value_block_indices = value_block_indices.reshape(block_count, SLOTS * BLOCK, HEAD_SIZE)
    gradient_per_block = grad_head.astype(jnp.float32).reshape(block_count, BLOCK, HEAD_SIZE)
    attention_logits = jnp.einsum('vrz,vsz->vrs', blocked_queries, key_block_indices) * logit_scale
    highest = lax.optimization_barrier(jnp.max(attention_logits, axis=-1, keepdims=True))
    expo = jnp.exp(attention_logits - highest)
    attn_probs = expo / lax.optimization_barrier(jnp.sum(expo, axis=-1, keepdims=True))
    reduced_probabilities = rounded(attn_probs)
    attended = jnp.einsum('tlh,ths->tls', reduced_probabilities, value_block_indices).astype(jnp.bfloat16).reshape(SEQUENCE_LENGTH, HEAD_SIZE)
    value_contributions = jnp.einsum('uay,uax->uyx', reduced_probabilities, gradient_per_block)
    probability_gradient = jnp.einsum('vrz,vsz->vrs', gradient_per_block, value_block_indices)
    row_delta = lax.optimization_barrier(jnp.sum(attn_probs * probability_gradient, axis=-1, keepdims=True))
    score_gradient = rounded(attn_probs * (probability_gradient - row_delta) * logit_scale)
    query_gradient = jnp.einsum('tlh,ths->tls', score_gradient, key_block_indices).astype(jnp.bfloat16).reshape(SEQUENCE_LENGTH, HEAD_SIZE)
    key_contributions = jnp.einsum('uay,uax->uyx', score_gradient, blocked_queries)
    flat_ids = block_ids.reshape(-1).astype(jnp.int32)

    def collect(terms):
        summed = jax.ops.segment_sum(terms.reshape(block_count * SLOTS, BLOCK, HEAD_SIZE), flat_ids, num_segments=block_count)
        return summed.reshape(SEQUENCE_LENGTH, HEAD_SIZE).astype(jnp.bfloat16)
    return (attended, query_gradient, collect(key_contributions), collect(value_contributions))

def reference(query_rows, key_rows, value_rows, out_weight, grad_out, block_list):

    def split_heads(rows_in):
        return rows_in.reshape(SEQUENCE_LENGTH, HEADS, HEAD_SIZE).transpose(1, 0, 2)

    def join_heads(heads_in):
        return heads_in.transpose(1, 0, 2).reshape(SEQUENCE_LENGTH, D)

    def one_sequence(weight_sum, items):
        query_seq, key_seq, value_seq, grad_seq, block_ids = items
        grad_att = jnp.dot(grad_seq, out_weight.T, preferred_element_type=jnp.float32).astype(jnp.bfloat16)
        results = jax.vmap(head_pass, in_axes=(0, 0, 0, 0, None))(split_heads(query_seq), split_heads(key_seq), split_heads(value_seq), split_heads(grad_att), block_ids)
        attended = join_heads(results[0])
        weight_sum = weight_sum + jnp.dot(attended.T, grad_seq, preferred_element_type=jnp.float32)
        return (weight_sum, (attended, join_heads(results[1]), join_heads(results[2]), join_heads(results[3])))
    start_sum = jnp.zeros((D, D), jnp.float32)
    grad_weight, stacked = lax.scan(one_sequence, start_sum, (query_rows, key_rows, value_rows, grad_out, block_list))
    return (stacked[0], stacked[1], stacked[2], stacked[3], grad_weight)
```

```python
import functools
import math

import jax
import jax.numpy as jnp
from jax import lax
from jax.experimental import pallas as pl
from jax.experimental.pallas import tpu as pltpu
from jax.sharding import PartitionSpec as P

MESH = pl.DeviceIdType.MESH
F32, BF16 = jnp.float32, jnp.bfloat16
SEQ_LEN, HEADS, HEAD, BLOCK, WIDTH = 2048, 16, 128, 64, 2048
ROWS = SEQ_LEN // 16
NX, NY, NZ = 4, 8, 8
OFFSETS = (0, -1, 1, -2, 2, -3, 3, 4)


class Place:
    def __init__(self):
        self.dp = lax.axis_index("dp")
        self.seq = lax.axis_index("seq")
        self.y_hi = self.dp // 8
        self.x = (self.dp // 2) % 4
        self.core = self.dp % 2
        self.z = self.seq // 2
        self.y_lo = self.seq % 2
        self.y = 2 * self.y_hi + self.y_lo

    def dp_of(self, y_hi=None, x=None, core=None):
        y_hi = self.y_hi if y_hi is None else y_hi
        x = self.x if x is None else x
        core = self.core if core is None else core
        return y_hi * 8 + x * 2 + core

    def at_x(self, x):
        return (self.dp_of(x=x), self.seq)

    def at_y(self, y):
        return (self.dp_of(y_hi=y // 2), 2 * self.z + y % 2)

    def at_z(self, z):
        return (self.dp, 2 * z + self.y_lo)

    def at_seq(self, seq):
        return (self.dp, seq)

    def other_core(self):
        return (self.dp_of(core=1 - self.core), self.seq)


def greet(barrier, place, others):
    def one(d, _):
        to = place.at_seq((place.seq + d) % 16)
        pl.semaphore_signal(barrier, inc=1, device_id=to, device_id_type=MESH)
        return 0

    lax.fori_loop(1, 16, one, 0)
    for to in others:
        pl.semaphore_signal(barrier, inc=1, device_id=to, device_id_type=MESH)
    pl.semaphore_wait(barrier, 15 + len(others))


def remote(src, dst, send, recv, to):
    return pltpu.make_async_remote_copy(
        src_ref=src, dst_ref=dst, send_sem=send, recv_sem=recv, device_id=to, device_id_type=MESH
    )


def each(low, high, act):
    def one(i, _):
        act(i)
        return 0

    lax.fori_loop(low, high, one, 0)


def cols(i):
    return pl.ds(pl.multiple_of(i * HEAD, HEAD), HEAD)


def rows(i):
    return pl.ds(pl.multiple_of(i * ROWS, ROWS), ROWS)


def spread_kernel(
    q_ref, k_ref, v_ref, g_ref, w_ref, qh_ref, kh_ref, vh_ref, dh_ref,
    w_all, d_out, a_send, a_recv, own_sem, z_send, z_recv, y_send, y_recv, x_send, x_recv,
    f_send, f_recv, c_send, c_recv,
):
    here = Place()
    up = here.at_y((here.y + 1) % NY)
    down = here.at_y((here.y + NY - 1) % NY)
    right = here.at_x((here.x + 1) % NX)
    left = here.at_x((here.x + NX - 1) % NX)
    step = 2 * here.y_lo - 1
    far_y = here.at_y((here.y + NY + step) % NY)
    greet(pltpu.get_barrier_semaphore(), here, (far_y, right, left, here.other_core()))

    def moved(src, dst, a, d):
        return remote(
            src.at[:, cols((here.seq + d) % 16)], dst.at[rows(here.seq), :], a_send.at[a, d], a_recv.at[a, d],
            here.at_seq((here.seq + d) % 16),
        )

    def kept(src, dst, a):
        return pltpu.make_async_copy(src.at[:, cols(here.seq)], dst.at[rows(here.seq), :], own_sem.at[a])

    def weights(y, x=None, core=None, z=slice(None)):
        at = pl.multiple_of(here.dp_of(y // 2, x, core) * 64, 64)
        return w_all.at[y % 2, z, pl.ds(at, 64), :]

    own = w_all.at[here.y_lo, here.z, pl.ds(pl.multiple_of(here.dp * 64, 64), 64), :]
    own[...] = w_ref[...].astype(F32).T.astype(BF16)

    def along_z(d):
        return remote(own, own, z_send.at[d], z_recv.at[d], here.at_z((here.z + d) % NZ))

    each(1, NZ, lambda d: along_z(d).start())
    pairs = ((q_ref, qh_ref), (k_ref, kh_ref), (v_ref, vh_ref))
    for a, (src, dst) in enumerate(pairs):
        kept(src, dst, a).start()
        each(1, 16, lambda d: moved(src, dst, a, d).start())
    each(1, NZ, lambda d: along_z(d).wait_recv())

    def along_y(way, k):
        sign = 1 if way == 0 else -1
        half = slice(None) if k < 3 else (pl.ds(0, 4) if way == 0 else pl.ds(4, 4))
        block = weights((here.y - sign * k + NY) % NY, z=half)
        return remote(block, block, y_send.at[way, k], y_recv.at[way, k], up if way == 0 else down)

    def along_x(way, j):
        block = weights((here.y + OFFSETS[j] + NY) % NY)
        return remote(block, block, x_send.at[way, j], x_recv.at[way, j], right if way == 0 else left)

    def from_x(way, j):
        x = (here.x + (NX - 1 if way == 0 else 1)) % NX
        block = weights((here.y + OFFSETS[j] + NY) % NY, x)
        return remote(block, block, f_send.at[j], f_recv.at[j], right if way == 0 else left)

    def to_core(i, j):
        x = (here.x + i) % NX
        block = weights((here.y + OFFSETS[j] + NY) % NY, x)
        return remote(block, block, c_send.at[i, j], c_recv.at[i, j], here.other_core())

    def on(j):
        along_x(0, j).start()
        along_x(1, j).start()
        to_core(0, j).start()

    along_y(0, 0).start()
    along_y(1, 0).start()
    on(0)
    for k in range(3):
        for way in range(2):
            along_y(way, k).wait_recv()
            along_y(way, k + 1).start()
            on(1 + 2 * k + way)
    along_y(0, 3).wait_recv()
    along_y(1, 3).wait_recv()
    on(7)
    for j in range(8):
        for way in range(2):
            along_x(way, j).wait_recv()
            if j % 2 == way:
                from_x(way, j).start()
            to_core(3 if way == 0 else 1, j).start()
    for j in range(8):
        from_x(j % 2, j).wait_recv()
        to_core(2, j).start()
    for i in (0, 3, 1, 2):
        for j in range(8):
            to_core(i, j).wait_recv()

    def project(d):
        head = (here.seq + d) % 16
        w = w_all[head % 2, head // 2]
        d_out[head] = jnp.dot(g_ref[...], w, preferred_element_type=F32).astype(BF16)

    def sent(d):
        head = (here.seq + d) % 16
        return remote(
            d_out.at[head], dh_ref.at[rows(here.seq), :], a_send.at[3, d], a_recv.at[3, d], here.at_seq(head)
        )

    def project_and_send(d):
        project(d)
        sent(d).start()

    each(1, 16, project_and_send)
    project(0)
    own_d = pltpu.make_async_copy(d_out.at[here.seq], dh_ref.at[rows(here.seq), :], own_sem.at[3])
    own_d.start()

    for a, (src, dst) in enumerate(pairs):
        kept(src, dst, a).wait()
        each(1, 16, lambda d: moved(src, dst, a, d).wait())
    own_d.wait()
    each(1, 16, lambda d: sent(d).wait())
    each(1, NZ, lambda d: along_z(d).wait_send())
    for way in range(2):
        for k in range(4):
            along_y(way, k).wait_send()
        for j in range(8):
            along_x(way, j).wait_send()
    for j in range(8):
        from_x(j % 2, j).wait_send()
        for i in range(4):
            to_core(i, j).wait_send()


def spread(q, k, v, g, w):
    flat = jax.ShapeDtypeStruct((SEQ_LEN, HEAD), BF16)
    any_, vmem = pl.BlockSpec(memory_space=pl.ANY), pl.BlockSpec(memory_space=pltpu.VMEM)
    dma = pltpu.SemaphoreType.DMA
    return pl.pallas_call(
        spread_kernel,
        out_shape=(flat,) * 4,
        in_specs=[any_, any_, any_, vmem, vmem],
        out_specs=(any_,) * 4,
        scratch_shapes=[
            pltpu.VMEM((2, NZ, WIDTH, HEAD), BF16),
            pltpu.VMEM((HEADS, ROWS, HEAD), BF16),
            dma((4, 16)), dma((4, 16)), dma((4,)), dma((NZ,)), dma((NZ,)), dma((2, 4)), dma((2, 4)),
            dma((2, 8)), dma((2, 8)), dma((8,)), dma((8,)), dma((4, 8)), dma((4, 8)),
        ],
        compiler_params=pltpu.CompilerParams(
            collective_id=0, has_side_effects=True, vmem_limit_bytes=40 * 2**20
        ),
        name="spread",
    )(q, k, v, g, w)


def attention_kernel(ids_ref, q_ref, k_ref, v_ref, d_ref, att_ref, dq_ref, dk_ref, dv_ref, dk_sum, dv_sum):
    scale = 1.0 / math.sqrt(HEAD)
    slots = ids_ref.shape[1]
    dk_sum[...] = jnp.zeros_like(dk_sum)
    dv_sum[...] = jnp.zeros_like(dv_sum)

    def dot(a, b, i, j):
        return lax.dot_general(a, b, (((i,), (j,)), ((), ())), preferred_element_type=F32)

    def one(b):
        here = pl.ds(pl.multiple_of(b * BLOCK, BLOCK), BLOCK)
        at = [pl.ds(pl.multiple_of(ids_ref[b, s] * BLOCK, BLOCK), BLOCK) for s in range(slots)]
        q, d = q_ref[here, :], d_ref[here, :]
        k = jnp.concatenate([k_ref[i, :] for i in at], axis=0)
        v = jnp.concatenate([v_ref[i, :] for i in at], axis=0)
        logits = dot(q, k, 1, 1) * scale
        expo = jnp.exp(logits - jnp.max(logits, axis=1, keepdims=True))
        probs = expo / jnp.sum(expo, axis=1, keepdims=True)
        low = probs.astype(BF16)
        att_ref[here, :] = dot(low, v, 1, 0).astype(BF16)
        d_probs = dot(d, v, 1, 1)
        delta = jnp.sum(probs * d_probs, axis=1, keepdims=True)
        d_logits = (probs * (d_probs - delta) * scale).astype(BF16)
        dq_ref[here, :] = dot(d_logits, k, 1, 0).astype(BF16)
        dk, dv = dot(d_logits, q, 0, 0), dot(low, d, 0, 0)
        for s in range(slots):
            dk_sum[at[s], :] += dk[s * BLOCK : (s + 1) * BLOCK]
            dv_sum[at[s], :] += dv[s * BLOCK : (s + 1) * BLOCK]

    each(0, SEQ_LEN // BLOCK, one)
    dk_ref[...] = dk_sum[...].astype(BF16)
    dv_ref[...] = dv_sum[...].astype(BF16)


def attention(ids, q, k, v, d):
    flat = jax.ShapeDtypeStruct((SEQ_LEN, HEAD), BF16)
    vmem = pl.BlockSpec(memory_space=pltpu.VMEM)
    return pl.pallas_call(
        attention_kernel,
        out_shape=(flat,) * 4,
        in_specs=[pl.BlockSpec(memory_space=pltpu.SMEM)] + [vmem] * 4,
        out_specs=(vmem,) * 4,
        scratch_shapes=[pltpu.VMEM((SEQ_LEN, HEAD), F32)] * 2,
        compiler_params=pltpu.CompilerParams(vmem_limit_bytes=40 * 2**20),
        name="attention",
    )(ids, q, k, v, d)


def collect_kernel(
    ah_ref, qh_ref, kh_ref, vh_ref, g_ref, att_ref, dq_ref, dk_ref, dv_ref, gw_ref,
    att4, g4, product, c_out, c_in, y_out, y_in, z_out, z_in, last_out, last_in,
    a_send, a_recv, own_sem, g_send, g_recv, x_send, x_recv, f_send, f_recv, c_send, c_recv,
    y_send, y_recv, z_send, z_recv, att_sem,
):
    here = Place()
    right = here.at_x((here.x + 1) % NX)
    left = here.at_x((here.x + NX - 1) % NX)
    others = [here.at_x((here.x + d) % NX) for d in range(1, NX)]
    for d in range(1, 4):
        for y_lo in range(2):
            others.append((here.dp_of(y_hi=(here.y_hi + d) % 4), 2 * here.z + y_lo))
    others.append(here.other_core())
    greet(pltpu.get_barrier_semaphore(), here, others)

    mine = att4.at[here.x]

    def moved(src, dst, a, d):
        to = (here.seq + d) % 16
        return remote(
            src.at[rows(to), :], dst.at[:, cols(here.seq)], a_send.at[a, d], a_recv.at[a, d], here.at_seq(to)
        )

    def kept(src, dst, a):
        return pltpu.make_async_copy(src.at[rows(here.seq), :], dst.at[:, cols(here.seq)], own_sem.at[a])

    def grads(d, y_hi):
        x = (here.x + d) % NX
        return remote(
            g_ref.at[:, cols(y_hi * NX + x)], g4.at[here.x, :, cols(y_hi)], g_send.at[d, y_hi], g_recv.at[d, y_hi],
            here.at_x(x),
        )

    def own_grads(y_hi):
        return pltpu.make_async_copy(
            g_ref.at[:, cols(y_hi * NX + here.x)], g4.at[here.x, :, cols(y_hi)], g_send.at[0, y_hi]
        )

    pairs = ((ah_ref, mine), (qh_ref, dq_ref), (kh_ref, dk_ref), (vh_ref, dv_ref))
    for a, (src, dst) in enumerate(pairs):
        kept(src, dst, a).start()
        each(1, 16, lambda d: moved(src, dst, a, d).start())
        if a == 0:
            for y_hi in range(4):
                own_grads(y_hi).start()
                each(1, NX, lambda d: grads(d, y_hi).start())

    kept(ah_ref, mine, 0).wait()
    each(1, 16, lambda d: moved(ah_ref, mine, 0, d).wait_recv())
    att_copy = pltpu.make_async_copy(mine, att_ref, att_sem)
    att_copy.start()

    def half(part, x):
        return att4.at[x, :, pl.ds(part * (WIDTH // 2), WIDTH // 2)]

    def along_x(way, part):
        block = half(part, here.x)
        return remote(block, block, x_send.at[way, part], x_recv.at[way, part], right if way == 0 else left)

    def forward(way):
        block = half(way, (here.x + (NX - 1 if way == 0 else 1)) % NX)
        return remote(block, block, f_send.at[way], f_recv.at[way], right if way == 0 else left)

    for part in range(2):
        along_x(0, part).start()
        along_x(1, 1 - part).start()
    for way in range(2):
        along_x(way, way).wait_recv()
        forward(way).start()
    for way in range(2):
        along_x(way, 1 - way).wait_recv()
    for way in range(2):
        forward(way).wait_recv()
    for y_hi in range(4):
        own_grads(y_hi).wait()
        each(1, NX, lambda d: grads(d, y_hi).wait_recv())

    def multiply(h):
        a = att4[:, :, cols(h)].reshape(NX * ROWS, HEAD)
        total = lax.dot_general(
            a, g4[...].reshape(NX * ROWS, 4 * HEAD), (((0,), (0,)), ((), ())), preferred_element_type=F32
        )
        product[h] = total
        c_out[h] = total.astype(BF16)

    each(0, HEADS, multiply)

    def half_rows(core):
        return pl.ds(pl.multiple_of(core * 64, 64), 64)

    to_core = remote(
        c_out.at[:, half_rows(1 - here.core), :], c_in, c_send.at[0], c_recv.at[0], here.other_core()
    )
    to_core.start()
    to_core.wait()

    def add_core(h):
        total = product[h, half_rows(here.core), :] + c_in[h].astype(F32)
        for y_hi in range(4):
            y_out[y_hi * 2 + h % 2, h // 2] = total[:, y_hi * HEAD : (y_hi + 1) * HEAD].astype(BF16)

    each(0, HEADS, add_core)

    def along_y(d):
        y = (here.y + d) % NY
        return remote(y_out.at[y], y_in.at[d], y_send.at[d], y_recv.at[d], here.at_y(y))

    each(1, NY, lambda d: along_y(d).start())
    each(1, NY, lambda d: along_y(d).wait())

    def add_y(z):
        total = y_out[here.y, z].astype(F32)
        for d in range(1, NY):
            total += y_in[d, z].astype(F32)
        z_out[z] = total.astype(BF16)

    each(0, NZ, add_y)

    def along_z(d):
        z = (here.z + d) % NZ
        return remote(z_out.at[z], z_in.at[d], z_send.at[d], z_recv.at[d], here.at_z(z))

    each(1, NZ, lambda d: along_z(d).start())
    each(1, NZ, lambda d: along_z(d).wait())
    total = z_out[here.z].astype(F32)
    for d in range(1, NZ):
        total += z_in[d].astype(F32)
    last_out[...] = total
    swap = remote(last_out, last_in, c_send.at[1], c_recv.at[1], here.other_core())
    swap.start()
    swap.wait()
    first = here.core == 0
    top = jnp.where(first, last_out[...], last_in[...])
    bottom = jnp.where(first, last_in[...], last_out[...])
    gw_ref[:64, :] = jnp.where(first, top[:, :64], top[:, 64:])
    gw_ref[64:, :] = jnp.where(first, bottom[:, :64], bottom[:, 64:])

    att_copy.wait()
    for way in range(2):
        for part in range(2):
            along_x(way, part).wait_send()
        forward(way).wait_send()
    for y_hi in range(4):
        each(1, NX, lambda d: grads(d, y_hi).wait_send())
    each(1, 16, lambda d: moved(ah_ref, mine, 0, d).wait_send())
    for a, (src, dst) in enumerate(pairs):
        if a > 0:
            kept(src, dst, a).wait()
            each(1, 16, lambda d: moved(src, dst, a, d).wait())


def collect(att, dq, dk, dv, g):
    flat = jax.ShapeDtypeStruct((ROWS, WIDTH), BF16)
    any_, vmem = pl.BlockSpec(memory_space=pl.ANY), pl.BlockSpec(memory_space=pltpu.VMEM)
    dma = pltpu.SemaphoreType.DMA
    return pl.pallas_call(
        collect_kernel,
        out_shape=(flat,) * 4 + (jax.ShapeDtypeStruct((HEAD, 64), F32),),
        in_specs=[any_] * 5,
        out_specs=(any_,) * 4 + (vmem,),
        scratch_shapes=[
            pltpu.VMEM((NX, ROWS, WIDTH), BF16),
            pltpu.VMEM((NX, ROWS, 4 * HEAD), BF16),
            pltpu.VMEM((HEADS, HEAD, 4 * HEAD), F32),
            pltpu.VMEM((HEADS, HEAD, 4 * HEAD), BF16),
            pltpu.VMEM((HEADS, 64, 4 * HEAD), BF16),
            pltpu.VMEM((NY, NZ, 64, HEAD), BF16),
            pltpu.VMEM((NY, NZ, 64, HEAD), BF16),
            pltpu.VMEM((NZ, 64, HEAD), BF16),
            pltpu.VMEM((NZ, 64, HEAD), BF16),
            pltpu.VMEM((64, HEAD), F32),
            pltpu.VMEM((64, HEAD), F32),
            dma((4, 16)), dma((4, 16)), dma((4,)), dma((4, 4)), dma((4, 4)), dma((2, 2)), dma((2, 2)),
            dma((2,)), dma((2,)), dma((2,)), dma((2,)), dma((NY,)), dma((NY,)), dma((NZ,)), dma((NZ,)),
            dma,
        ],
        compiler_params=pltpu.CompilerParams(
            collective_id=1, has_side_effects=True, vmem_limit_bytes=40 * 2**20
        ),
        name="collect",
    )(att, dq, dk, dv, g)


def local(query_rows, key_rows, value_rows, out_weight, grad_out, block_list):
    heads = spread(query_rows[0], key_rows[0], value_rows[0], grad_out[0], out_weight)
    results = attention(block_list[0], *heads)
    att, dq, dk, dv, grad_weight = collect(*results, grad_out[0])
    return (att[None], dq[None], dk[None], dv[None], grad_weight)


def solution(mesh):
    return jax.shard_map(
        local,
        mesh=mesh,
        in_specs=(
            P("dp", "seq", None),
            P("dp", "seq", None),
            P("dp", "seq", None),
            P("seq", "dp"),
            P("dp", "seq", None),
            P("dp", None, None),
        ),
        out_specs=(
            P("dp", "seq", None),
            P("dp", "seq", None),
            P("dp", "seq", None),
            P("dp", "seq", None),
            P("seq", "dp"),
        ),
        check_vma=False,
    )
```

```python
import functools
import math

import jax
import jax.numpy as jnp
from jax import lax
from jax.experimental import pallas as pl
from jax.experimental.pallas import tpu as pltpu
from jax.sharding import PartitionSpec as P

MESH = pl.DeviceIdType.MESH
F32, BF16 = jnp.float32, jnp.bfloat16
SEQ_LEN, HEADS, HEAD, BLOCK, WIDTH = 2048, 16, 128, 64, 2048
ROWS = SEQ_LEN // 16
NX, NY, NZ = 4, 8, 8
OFFSETS = (0, -1, 1, -2, 2, -3, 3, 4)


SAME_Y, OTHER_Y = (8, 6, 10, 4, 12, 2, 14), (7, 9, 5, 11, 3, 13, 1, 15)


class Queue:
    def __init__(self, copies):
        self.copies = list(copies)

    def start(self, count):
        for make, *args in self.copies[:count]:
            make(*args).start()
        self.copies = self.copies[count:]


class Place:
    def __init__(self):
        self.dp = lax.axis_index("dp")
        self.seq = lax.axis_index("seq")
        self.y_hi = self.dp // 8
        self.x = (self.dp // 2) % 4
        self.core = self.dp % 2
        self.z = self.seq // 2
        self.y_lo = self.seq % 2
        self.y = 2 * self.y_hi + self.y_lo

    def dp_of(self, y_hi=None, x=None, core=None):
        y_hi = self.y_hi if y_hi is None else y_hi
        x = self.x if x is None else x
        core = self.core if core is None else core
        return y_hi * 8 + x * 2 + core

    def at_x(self, x):
        return (self.dp_of(x=x), self.seq)

    def at_y(self, y):
        return (self.dp_of(y_hi=y // 2), 2 * self.z + y % 2)

    def at_z(self, z):
        return (self.dp, 2 * z + self.y_lo)

    def at_seq(self, seq):
        return (self.dp, seq)

    def other_core(self):
        return (self.dp_of(core=1 - self.core), self.seq)


def greet(barrier, place, others):
    def one(d, _):
        to = place.at_seq((place.seq + d) % 16)
        pl.semaphore_signal(barrier, inc=1, device_id=to, device_id_type=MESH)
        return 0

    lax.fori_loop(1, 16, one, 0)
    for to in others:
        pl.semaphore_signal(barrier, inc=1, device_id=to, device_id_type=MESH)
    pl.semaphore_wait(barrier, 15 + len(others))


def remote(src, dst, send, recv, to):
    return pltpu.make_async_remote_copy(
        src_ref=src, dst_ref=dst, send_sem=send, recv_sem=recv, device_id=to, device_id_type=MESH
    )


def each(low, high, act):
    def one(i, _):
        act(i)
        return 0

    lax.fori_loop(low, high, one, 0)


def cols(i):
    return pl.ds(pl.multiple_of(i * HEAD, HEAD), HEAD)


def rows(i):
    return pl.ds(pl.multiple_of(i * ROWS, ROWS), ROWS)


def dot(a, b, i, j):
    return lax.dot_general(a, b, (((i,), (j,)), ((), ())), preferred_element_type=F32)


def block(b):
    return pl.ds(pl.multiple_of(b * BLOCK, BLOCK), BLOCK)


SLOTS = 8
SCALE = 1.0 / math.sqrt(HEAD)
TOGETHER = 4


def listed(ids_ref, b):
    return [ids_ref[b, s] for s in range(SLOTS)]


def gathered(ref, at):
    return jnp.concatenate([ref[i] for i in at], axis=0)


FLAT = jax.ShapeDtypeStruct((SEQ_LEN, HEAD), BF16)
BLOCKED = jax.ShapeDtypeStruct((SEQ_LEN // BLOCK, BLOCK, HEAD), BF16)
PROBS = jax.ShapeDtypeStruct((SEQ_LEN // BLOCK, BLOCK, SLOTS * BLOCK), F32)
VMEM = pl.BlockSpec(memory_space=pltpu.VMEM)


def outward_kernel(
    ids_ref, q_ref, k_ref, v_ref, g_ref, w_ref, qh_ref, kh_ref, vh_ref, dh_ref, probs_ref, att_ref, att4, g4,
    w_all, att_out, d_out, a_send, a_recv, own_sem, z_send, z_recv, y_send, y_recv, x_send, x_recv,
    f_send, f_recv, c_send, c_recv, g_send, g_recv, m_send, m_recv, n_send, n_recv,
):
    here = Place()
    up = here.at_y((here.y + 1) % NY)
    down = here.at_y((here.y + NY - 1) % NY)
    right = here.at_x((here.x + 1) % NX)
    left = here.at_x((here.x + NX - 1) % NX)
    far_y = here.at_y((here.y + NY + 2 * here.y_lo - 1) % NY)
    others = [here.at_x((here.x + d) % NX) for d in range(1, NX)]
    greet(pltpu.get_barrier_semaphore(), here, [far_y, here.other_core()] + others)
    mine = att4.at[here.x]

    def seq_at(d):
        return (here.seq + d) % 16

    def moved(src, dst, a, d):
        return remote(
            src.at[:, :, cols(seq_at(d))], dst.at[pl.ds(2 * here.seq, 2)], a_send.at[a, d], a_recv.at[a, d],
            here.at_seq(seq_at(d)),
        )

    def kept(src, dst, a):
        return pltpu.make_async_copy(src.at[:, :, cols(here.seq)], dst.at[pl.ds(2 * here.seq, 2)], own_sem.at[a])

    def arrived(src, dst, a):
        kept(src, dst, a).wait()
        each(1, 16, lambda d: moved(src, dst, a, d).wait_recv())

    def weights(y, x=None, z=slice(None)):
        at = pl.multiple_of(here.dp_of(y // 2, x) * 64, 64)
        return w_all.at[y % 2, z, pl.ds(at, 64), :]

    own = w_all.at[here.y_lo, here.z, pl.ds(pl.multiple_of(here.dp * 64, 64), 64), :]
    own[...] = w_ref[...].astype(F32).T.astype(BF16)

    def along_z(d):
        return remote(own, own, z_send.at[d], z_recv.at[d], here.at_z((here.z + d) % NZ))

    def along_y(way, k):
        sign = 1 if way == 0 else -1
        part = slice(None) if k < 3 else (pl.ds(0, 4) if way == 0 else pl.ds(4, 4))
        at = weights((here.y - sign * k + NY) % NY, z=part)
        return remote(at, at, y_send.at[way, k], y_recv.at[way, k], up if way == 0 else down)

    def along_x(way, j):
        at = weights((here.y + OFFSETS[j] + NY) % NY)
        return remote(at, at, x_send.at[way, j], x_recv.at[way, j], right if way == 0 else left)

    def from_x(way, j):
        x = (here.x + (NX - 1 if way == 0 else 1)) % NX
        at = weights((here.y + OFFSETS[j] + NY) % NY, x)
        return remote(at, at, f_send.at[j], f_recv.at[j], right if way == 0 else left)

    def to_core(i, j):
        at = weights((here.y + OFFSETS[j] + NY) % NY, (here.x + i) % NX)
        return remote(at, at, c_send.at[i, j], c_recv.at[i, j], here.other_core())

    def on(j):
        along_x(0, j).start()
        along_x(1, j).start()
        to_core(0, j).start()

    def grads(d, y_hi):
        x = (here.x + d) % NX
        return remote(
            g_ref.at[:, cols(y_hi * NX + x)], g4.at[here.x, :, cols(y_hi)], g_send.at[d, y_hi], g_recv.at[d, y_hi],
            here.at_x(x),
        )

    def own_grads(y_hi):
        return pltpu.make_async_copy(
            g_ref.at[:, cols(y_hi * NX + here.x)], g4.at[here.x, :, cols(y_hi)], g_send.at[0, y_hi]
        )

    def att(d):
        to = seq_at(d)
        return remote(
            att_out.at[rows(to), :], mine.at[:, cols(here.seq)], a_send.at[3, d], a_recv.at[3, d], here.at_seq(to)
        )

    own_att = pltpu.make_async_copy(att_out.at[rows(here.seq), :], mine.at[:, cols(here.seq)], own_sem.at[3])

    def d_att(d):
        to = seq_at(d)
        return remote(d_out.at[to], dh_ref.at[rows(here.seq), :], a_send.at[4, d], a_recv.at[4, d], here.at_seq(to))

    own_d = pltpu.make_async_copy(d_out.at[here.seq], dh_ref.at[rows(here.seq), :], own_sem.at[4])

    def half(part, x):
        return att4.at[x, :, pl.ds(part * (WIDTH // 2), WIDTH // 2)]

    def att_x(way, part):
        at = half(part, here.x)
        return remote(at, at, m_send.at[way, part], m_recv.at[way, part], right if way == 0 else left)

    def att_onward(way):
        at = half(way, (here.x + (NX - 1 if way == 0 else 1)) % NX)
        return remote(at, at, n_send.at[way], n_recv.at[way], right if way == 0 else left)

    pairs = ((q_ref, qh_ref), (k_ref, kh_ref), (v_ref, vh_ref))
    order = [(0, SAME_Y), (1, SAME_Y), (0, OTHER_Y), (1, OTHER_Y), (2, SAME_Y), (2, OTHER_Y)]
    queue = Queue((moved, *pairs[a], a, d) for a, ds in order for d in ds)
    each(1, NZ, lambda d: along_z(d).start())
    queue.start(14)
    for a, (src, dst) in enumerate(pairs):
        kept(src, dst, a).start()
    each(1, NZ, lambda d: along_z(d).wait_recv())
    along_y(0, 0).start()
    along_y(1, 0).start()
    on(0)
    for k in range(3):
        for way in range(2):
            along_y(way, k).wait_recv()
            along_y(way, k + 1).start()
            on(1 + 2 * k + way)
            queue.start(3)
    along_y(0, 3).wait_recv()
    along_y(1, 3).wait_recv()
    on(7)

    def next_x(j):
        for way in range(2):
            along_x(way, j).wait_recv()
            if j % 2 == way:
                from_x(way, j).start()
            queue.start(2)
            to_core(3 if way == 0 else 1, j).start()

    for j in range(4):
        next_x(j)

    arrived(*pairs[0], 0)
    arrived(*pairs[1], 1)

    def softmax(step):
        blocks = [step * TOGETHER + i for i in range(TOGETHER)]
        logits = [dot(qh_ref[b], gathered(kh_ref, listed(ids_ref, b)), 1, 1) * SCALE for b in blocks]
        expo = [jnp.exp(x - jnp.max(x, axis=1, keepdims=True)) for x in logits]
        for b, x in zip(blocks, expo):
            probs_ref[b] = x / jnp.sum(x, axis=1, keepdims=True)

    steps = SEQ_LEN // BLOCK // TOGETHER // 4
    for j in range(4):
        each(j * steps, (j + 1) * steps, softmax)
        next_x(4 + j)
    arrived(*pairs[2], 2)

    def attend(chunks):
        blocks = [2 * c + i for c in chunks for i in range(2)]
        out = [dot(probs_ref[b].astype(BF16), gathered(vh_ref, listed(ids_ref, b)), 1, 0) for b in blocks]
        for b, x in zip(blocks, out):
            att_out[block(b), :] = x.astype(BF16)

    def attend_and_send(i):
        attend([seq_at(2 * i + 1), seq_at(2 * i + 2)])
        att(2 * i + 1).start()
        att(2 * i + 2).start()

    each(0, 7, attend_and_send)
    attend([seq_at(15), here.seq])
    att(15).start()
    own_att.start()
    for j in range(8):
        from_x(j % 2, j).wait_recv()
        to_core(2, j).start()
    for y_hi in range(4):
        own_grads(y_hi).start()
        each(1, NX, lambda d: grads(d, y_hi).start())
    for i in (0, 3, 1, 2):
        for j in range(8):
            to_core(i, j).wait_recv()

    def project(head):
        d_out[head] = jnp.dot(g_ref[...], w_all[head % 2, head // 2], preferred_element_type=F32).astype(BF16)

    def project_and_send(d):
        project(seq_at(d))
        d_att(d).start()

    each(1, 16, project_and_send)
    project(here.seq)
    own_d.start()

    own_att.wait()
    each(1, 16, lambda d: att(d).wait_recv())
    att_copy = pltpu.make_async_copy(mine, att_ref, own_sem.at[5])
    att_copy.start()
    for part in range(2):
        att_x(0, part).start()
        att_x(1, 1 - part).start()
    for way in range(2):
        att_x(way, way).wait_recv()
        att_onward(way).start()
    for way in range(2):
        att_x(way, 1 - way).wait_recv()
    for way in range(2):
        att_onward(way).wait()
    for y_hi in range(4):
        own_grads(y_hi).wait()
        each(1, NX, lambda d: grads(d, y_hi).wait())
    own_d.wait()
    each(1, 16, lambda d: d_att(d).wait())
    att_copy.wait()

    for a, (src, dst) in enumerate(pairs):
        each(1, 16, lambda d: moved(src, dst, a, d).wait_send())
    each(1, 16, lambda d: att(d).wait_send())
    each(1, NZ, lambda d: along_z(d).wait_send())
    for way in range(2):
        for k in range(4):
            along_y(way, k).wait_send()
        for j in range(8):
            along_x(way, j).wait_send()
        for part in range(2):
            att_x(way, part).wait_send()
    for j in range(8):
        from_x(j % 2, j).wait_send()
        for i in range(4):
            to_core(i, j).wait_send()


def outward(ids, q, k, v, g, w):
    any_ = pl.BlockSpec(memory_space=pl.ANY)
    dma = pltpu.SemaphoreType.DMA
    return pl.pallas_call(
        outward_kernel,
        out_shape=(BLOCKED,) * 3
        + (
            FLAT,
            PROBS,
            jax.ShapeDtypeStruct((ROWS, WIDTH), BF16),
            jax.ShapeDtypeStruct((NX, ROWS, WIDTH), BF16),
            jax.ShapeDtypeStruct((NX, ROWS, 4 * HEAD), BF16),
        ),
        in_specs=[pl.BlockSpec(memory_space=pltpu.SMEM)] + [any_] * 3 + [VMEM] * 2,
        out_specs=(VMEM,) * 5 + (any_,) * 3,
        scratch_shapes=[
            pltpu.VMEM((2, NZ, WIDTH, HEAD), BF16),
            pltpu.VMEM((SEQ_LEN, HEAD), BF16),
            pltpu.VMEM((HEADS, ROWS, HEAD), BF16),
            dma((5, 16)), dma((5, 16)), dma((6,)), dma((NZ,)), dma((NZ,)), dma((2, 4)), dma((2, 4)),
            dma((2, 8)), dma((2, 8)), dma((8,)), dma((8,)), dma((4, 8)), dma((4, 8)),
            dma((4, 4)), dma((4, 4)), dma((2, 2)), dma((2, 2)), dma((2,)), dma((2,)),
        ],
        compiler_params=pltpu.CompilerParams(
            collective_id=0, has_side_effects=True, vmem_limit_bytes=44 * 2**20
        ),
        name="outward",
    )(ids, q, k, v, g, w)


def backward_kernel(ids_ref, q_ref, k_ref, v_ref, d_ref, probs_ref, dq_ref, dk_ref, dv_ref, dk_sum, dv_sum):
    dk_sum[...] = jnp.zeros_like(dk_sum)
    dv_sum[...] = jnp.zeros_like(dv_sum)

    def some(step):
        blocks = [step * TOGETHER + i for i in range(TOGETHER)]
        at = [listed(ids_ref, b) for b in blocks]
        d = [d_ref[block(b), :] for b in blocks]
        probs = [probs_ref[b] for b in blocks]
        d_probs = [dot(x, gathered(v_ref, i), 1, 1) for x, i in zip(d, at)]
        delta = [jnp.sum(x * y, axis=1, keepdims=True) for x, y in zip(probs, d_probs)]
        d_logits = [(x * (y - z) * SCALE).astype(BF16) for x, y, z in zip(probs, d_probs, delta)]
        dq = [dot(x, gathered(k_ref, i), 1, 0) for x, i in zip(d_logits, at)]
        dk = [dot(x, q_ref[b], 0, 0) for x, b in zip(d_logits, blocks)]
        dv = [dot(x.astype(BF16), y, 0, 0) for x, y in zip(probs, d)]
        for b, x in zip(blocks, dq):
            dq_ref[block(b), :] = x.astype(BF16)
        for i, x, y in zip(at, dk, dv):
            for s in range(SLOTS):
                dk_sum[block(i[s]), :] += x[s * BLOCK : (s + 1) * BLOCK]
                dv_sum[block(i[s]), :] += y[s * BLOCK : (s + 1) * BLOCK]

    each(0, SEQ_LEN // BLOCK // TOGETHER, some)
    dk_ref[...] = dk_sum[...].astype(BF16)
    dv_ref[...] = dv_sum[...].astype(BF16)


def backward(ids, q, k, v, d, probs):
    return pl.pallas_call(
        backward_kernel,
        out_shape=(FLAT,) * 3,
        in_specs=[pl.BlockSpec(memory_space=pltpu.SMEM)] + [VMEM] * 5,
        out_specs=(VMEM,) * 3,
        scratch_shapes=[pltpu.VMEM((SEQ_LEN, HEAD), F32)] * 2,
        compiler_params=pltpu.CompilerParams(vmem_limit_bytes=32 * 2**20),
        name="backward",
    )(ids, q, k, v, d, probs)


def collect_kernel(
    qh_ref, kh_ref, vh_ref, att4, g4, dq_ref, dk_ref, dv_ref, gw_ref,
    product, c_out, c_in, y_out, y_in, z_out, z_in, last_out, last_in,
    a_send, a_recv, own_sem, c_send, c_recv, y_send, y_recv, z_send, z_recv,
):
    here = Place()
    others = [here.other_core()]
    for d in range(1, 4):
        for y_lo in range(2):
            others.append((here.dp_of(y_hi=(here.y_hi + d) % 4), 2 * here.z + y_lo))
    greet(pltpu.get_barrier_semaphore(), here, others)

    def moved(src, dst, a, d):
        to = (here.seq + d) % 16
        return remote(
            src.at[rows(to), :], dst.at[:, cols(here.seq)], a_send.at[a, d], a_recv.at[a, d], here.at_seq(to)
        )

    def kept(src, dst, a):
        return pltpu.make_async_copy(src.at[rows(here.seq), :], dst.at[:, cols(here.seq)], own_sem.at[a])

    pairs = ((qh_ref, dq_ref), (kh_ref, dk_ref), (vh_ref, dv_ref))
    order = [(0, OTHER_Y), (0, SAME_Y), (1, SAME_Y), (2, SAME_Y), (1, OTHER_Y), (2, OTHER_Y)]
    queue = Queue((moved, *pairs[a], a, d) for a, ds in order for d in ds)
    queue.start(12)
    for a, (src, dst) in enumerate(pairs):
        kept(src, dst, a).start()

    def multiply(h):
        a = att4[:, :, cols(h)].reshape(NX * ROWS, HEAD)
        total = lax.dot_general(
            a, g4[...].reshape(NX * ROWS, 4 * HEAD), (((0,), (0,)), ((), ())), preferred_element_type=F32
        )
        product[h] = total
        c_out[h] = total.astype(BF16)

    each(0, HEADS, multiply)

    def half_rows(core):
        return pl.ds(pl.multiple_of(core * 64, 64), 64)

    to_core = remote(
        c_out.at[:, half_rows(1 - here.core), :], c_in, c_send.at[0], c_recv.at[0], here.other_core()
    )
    to_core.start()
    to_core.wait()

    def add_core(h):
        total = product[h, half_rows(here.core), :] + c_in[h].astype(F32)
        for y_hi in range(4):
            y_out[y_hi * 2 + h % 2, h // 2] = total[:, y_hi * HEAD : (y_hi + 1) * HEAD].astype(BF16)

    each(0, HEADS, add_core)

    def along_y(d):
        y = (here.y + d) % NY
        return remote(y_out.at[y], y_in.at[d], y_send.at[d], y_recv.at[d], here.at_y(y))

    each(1, NY, lambda d: along_y(d).start())
    queue.start(17)
    each(1, NY, lambda d: along_y(d).wait())

    def add_y(z):
        total = y_out[here.y, z].astype(F32)
        for d in range(1, NY):
            total += y_in[d, z].astype(F32)
        z_out[z] = total.astype(BF16)

    each(0, NZ, add_y)

    def along_z(d):
        z = (here.z + d) % NZ
        return remote(z_out.at[z], z_in.at[d], z_send.at[d], z_recv.at[d], here.at_z(z))

    each(1, NZ, lambda d: along_z(d).start())
    queue.start(16)
    each(1, NZ, lambda d: along_z(d).wait())
    total = z_out[here.z].astype(F32)
    for d in range(1, NZ):
        total += z_in[d].astype(F32)
    last_out[...] = total
    swap = remote(last_out, last_in, c_send.at[1], c_recv.at[1], here.other_core())
    swap.start()
    swap.wait()
    first = here.core == 0
    top = jnp.where(first, last_out[...], last_in[...])
    bottom = jnp.where(first, last_in[...], last_out[...])
    gw_ref[:64, :] = jnp.where(first, top[:, :64], top[:, 64:])
    gw_ref[64:, :] = jnp.where(first, bottom[:, :64], bottom[:, 64:])

    for a, (src, dst) in enumerate(pairs):
        kept(src, dst, a).wait()
        each(1, 16, lambda d: moved(src, dst, a, d).wait())


def collect(dq, dk, dv, att4, g4):
    flat = jax.ShapeDtypeStruct((ROWS, WIDTH), BF16)
    any_, vmem = pl.BlockSpec(memory_space=pl.ANY), pl.BlockSpec(memory_space=pltpu.VMEM)
    dma = pltpu.SemaphoreType.DMA
    return pl.pallas_call(
        collect_kernel,
        out_shape=(flat,) * 3 + (jax.ShapeDtypeStruct((HEAD, 64), F32),),
        in_specs=[any_] * 3 + [vmem] * 2,
        out_specs=(any_,) * 3 + (vmem,),
        scratch_shapes=[
            pltpu.VMEM((HEADS, HEAD, 4 * HEAD), F32),
            pltpu.VMEM((HEADS, HEAD, 4 * HEAD), BF16),
            pltpu.VMEM((HEADS, 64, 4 * HEAD), BF16),
            pltpu.VMEM((NY, NZ, 64, HEAD), BF16),
            pltpu.VMEM((NY, NZ, 64, HEAD), BF16),
            pltpu.VMEM((NZ, 64, HEAD), BF16),
            pltpu.VMEM((NZ, 64, HEAD), BF16),
            pltpu.VMEM((64, HEAD), F32),
            pltpu.VMEM((64, HEAD), F32),
            dma((3, 16)), dma((3, 16)), dma((3,)), dma((2,)), dma((2,)),
            dma((NY,)), dma((NY,)), dma((NZ,)), dma((NZ,)),
        ],
        compiler_params=pltpu.CompilerParams(
            collective_id=1, has_side_effects=True, vmem_limit_bytes=40 * 2**20
        ),
        name="collect",
    )(dq, dk, dv, att4, g4)


def in_blocks(flat):
    return flat.reshape(ROWS // BLOCK, BLOCK, WIDTH)


def local(query_rows, key_rows, value_rows, out_weight, grad_out, block_list):
    ids = block_list[0]
    q, k, v, d, probs, att, att4, g4 = outward(
        ids, in_blocks(query_rows), in_blocks(key_rows), in_blocks(value_rows), grad_out[0], out_weight
    )
    dq, dk, dv = backward(ids, q, k, v, d, probs)
    dq, dk, dv, grad_weight = collect(dq, dk, dv, att4, g4)
    return (att[None], dq[None], dk[None], dv[None], grad_weight)


def solution(mesh):
    return jax.shard_map(
        local,
        mesh=mesh,
        in_specs=(
            P("dp", "seq", None),
            P("dp", "seq", None),
            P("dp", "seq", None),
            P("seq", "dp"),
            P("dp", "seq", None),
            P("dp", None, None),
        ),
        out_specs=(
            P("dp", "seq", None),
            P("dp", "seq", None),
            P("dp", "seq", None),
            P("dp", "seq", None),
            P("seq", "dp"),
        ),
        check_vma=False,
    )
```

```python
import functools
import math

import jax
import jax.numpy as jnp
from jax import lax
from jax.experimental import pallas as pl
from jax.experimental.pallas import tpu as pltpu
from jax.sharding import PartitionSpec as P

MESH = pl.DeviceIdType.MESH
F32, BF16 = jnp.float32, jnp.bfloat16
SEQ_LEN, HEADS, HEAD, BLOCK, WIDTH = 2048, 16, 128, 64, 2048
ROWS = SEQ_LEN // 16
NX, NY, NZ = 4, 8, 8
OFFSETS = (0, -1, 1, -2, 2, -3, 3, 4)


SAME_Y, OTHER_Y = (8, 6, 10, 4, 12, 2, 14), (7, 9, 5, 11, 3, 13, 1, 15)


class Queue:
    def __init__(self, copies):
        self.copies = list(copies)

    def start(self, count):
        for make, *args in self.copies[:count]:
            make(*args).start()
        self.copies = self.copies[count:]


class Place:
    def __init__(self):
        self.dp = lax.axis_index("dp")
        self.seq = lax.axis_index("seq")
        self.y_hi = self.dp // 8
        self.x = (self.dp // 2) % 4
        self.core = self.dp % 2
        self.z = self.seq // 2
        self.y_lo = self.seq % 2
        self.y = 2 * self.y_hi + self.y_lo

    def dp_of(self, y_hi=None, x=None, core=None):
        y_hi = self.y_hi if y_hi is None else y_hi
        x = self.x if x is None else x
        core = self.core if core is None else core
        return y_hi * 8 + x * 2 + core

    def at_x(self, x):
        return (self.dp_of(x=x), self.seq)

    def at_y(self, y):
        return (self.dp_of(y_hi=y // 2), 2 * self.z + y % 2)

    def at_z(self, z):
        return (self.dp, 2 * z + self.y_lo)

    def at_seq(self, seq):
        return (self.dp, seq)

    def other_core(self):
        return (self.dp_of(core=1 - self.core), self.seq)


def greet(barrier, place, others):
    def one(d, _):
        to = place.at_seq((place.seq + d) % 16)
        pl.semaphore_signal(barrier, inc=1, device_id=to, device_id_type=MESH)
        return 0

    lax.fori_loop(1, 16, one, 0)
    for to in others:
        pl.semaphore_signal(barrier, inc=1, device_id=to, device_id_type=MESH)
    pl.semaphore_wait(barrier, 15 + len(others))


def remote(src, dst, send, recv, to):
    return pltpu.make_async_remote_copy(
        src_ref=src, dst_ref=dst, send_sem=send, recv_sem=recv, device_id=to, device_id_type=MESH
    )


def each(low, high, act):
    def one(i, _):
        act(i)
        return 0

    lax.fori_loop(low, high, one, 0)


def cols(i):
    return pl.ds(pl.multiple_of(i * HEAD, HEAD), HEAD)


def rows(i):
    return pl.ds(pl.multiple_of(i * ROWS, ROWS), ROWS)


def dot(a, b, i, j):
    return lax.dot_general(a, b, (((i,), (j,)), ((), ())), preferred_element_type=F32)


def block(b):
    return pl.ds(pl.multiple_of(b * BLOCK, BLOCK), BLOCK)


SLOTS = 8
SCALE = 1.0 / math.sqrt(HEAD)
TOGETHER = 4


def fixed(b):
    return [(b + 31) % 32, b, (b + 1) % 32, 0, 31]


def listed(ids_ref, b):
    return fixed(b) + [ids_ref[b, s] for s in range(5, SLOTS)]


def gathered(ref, at):
    return jnp.concatenate([ref[i] for i in at], axis=0)


VMEM = pl.BlockSpec(memory_space=pltpu.VMEM)


def layer_kernel(
    ids_ref, drawn_ref, q_ref, k_ref, v_ref, g_ref, w_ref, att_ref, dq_ref, dk_ref, dv_ref, gw_ref,
    qh_ref, kh_ref, vh_ref, dh_ref, probs_ref, att4, g4, w_all, att_out, d_out, q_out, k_out, v_out,
    k_sum, v_sum, k_drawn, v_drawn, product, p_out, p_in, y_out, y_in, z_out, z_in, last_out, last_in,
    a_send, a_recv, own_sem, z_send, z_recv, y_send, y_recv, x_send, x_recv,
    f_send, f_recv, c_send, c_recv, g_send, g_recv, m_send, m_recv, n_send, n_recv,
    b_send, b_recv, own_back, p_send, p_recv, s_send, s_recv, t_send, t_recv,
):
    here = Place()
    up = here.at_y((here.y + 1) % NY)
    down = here.at_y((here.y + NY - 1) % NY)
    right = here.at_x((here.x + 1) % NX)
    left = here.at_x((here.x + NX - 1) % NX)
    others = [here.other_core()] + [here.at_x((here.x + d) % NX) for d in range(1, NX)]
    for d in range(1, 4):
        for y_lo in range(2):
            others.append((here.dp_of(y_hi=(here.y_hi + d) % 4), 2 * here.z + y_lo))
    greet(pltpu.get_barrier_semaphore(), here, others)
    mine = att4.at[here.x]

    def seq_at(d):
        return (here.seq + d) % 16

    def moved(src, dst, a, d):
        return remote(
            src.at[:, :, cols(seq_at(d))], dst.at[pl.ds(2 * here.seq, 2)], a_send.at[a, d], a_recv.at[a, d],
            here.at_seq(seq_at(d)),
        )

    def kept(src, dst, a):
        return pltpu.make_async_copy(src.at[:, :, cols(here.seq)], dst.at[pl.ds(2 * here.seq, 2)], own_sem.at[a])

    def arrived(src, dst, a):
        kept(src, dst, a).wait()
        each(1, 16, lambda d: moved(src, dst, a, d).wait_recv())

    def weights(y, x=None, z=slice(None)):
        at = pl.multiple_of(here.dp_of(y // 2, x) * 64, 64)
        return w_all.at[y % 2, z, pl.ds(at, 64), :]

    own = w_all.at[here.y_lo, here.z, pl.ds(pl.multiple_of(here.dp * 64, 64), 64), :]
    own[...] = w_ref[...].astype(F32).T.astype(BF16)

    def along_z(d):
        return remote(own, own, z_send.at[d], z_recv.at[d], here.at_z((here.z + d) % NZ))

    def along_y(way, k):
        sign = 1 if way == 0 else -1
        part = slice(None) if k < 3 else (pl.ds(0, 4) if way == 0 else pl.ds(4, 4))
        at = weights((here.y - sign * k + NY) % NY, z=part)
        return remote(at, at, y_send.at[way, k], y_recv.at[way, k], up if way == 0 else down)

    def along_x(way, j):
        at = weights((here.y + OFFSETS[j] + NY) % NY)
        return remote(at, at, x_send.at[way, j], x_recv.at[way, j], right if way == 0 else left)

    def from_x(way, j):
        x = (here.x + (NX - 1 if way == 0 else 1)) % NX
        at = weights((here.y + OFFSETS[j] + NY) % NY, x)
        return remote(at, at, f_send.at[j], f_recv.at[j], right if way == 0 else left)

    def to_core(i, j):
        at = weights((here.y + OFFSETS[j] + NY) % NY, (here.x + i) % NX)
        return remote(at, at, c_send.at[i, j], c_recv.at[i, j], here.other_core())

    def on(j):
        along_x(0, j).start()
        along_x(1, j).start()
        to_core(0, j).start()

    def grads(d, y_hi):
        x = (here.x + d) % NX
        return remote(
            g_ref.at[:, cols(y_hi * NX + x)], g4.at[here.x, :, cols(y_hi)], g_send.at[d, y_hi], g_recv.at[d, y_hi],
            here.at_x(x),
        )

    def own_grads(y_hi):
        return pltpu.make_async_copy(
            g_ref.at[:, cols(y_hi * NX + here.x)], g4.at[here.x, :, cols(y_hi)], g_send.at[0, y_hi]
        )

    def att(d):
        to = seq_at(d)
        return remote(
            att_out.at[rows(to), :], mine.at[:, cols(here.seq)], a_send.at[3, d], a_recv.at[3, d], here.at_seq(to)
        )

    own_att = pltpu.make_async_copy(att_out.at[rows(here.seq), :], mine.at[:, cols(here.seq)], own_sem.at[3])

    def d_att(d):
        to = seq_at(d)
        return remote(d_out.at[to], dh_ref.at[rows(here.seq), :], a_send.at[4, d], a_recv.at[4, d], here.at_seq(to))

    own_d = pltpu.make_async_copy(d_out.at[here.seq], dh_ref.at[rows(here.seq), :], own_sem.at[4])

    def half(part, x):
        return att4.at[x, :, pl.ds(part * (WIDTH // 2), WIDTH // 2)]

    def att_x(way, part):
        at = half(part, here.x)
        return remote(at, at, m_send.at[way, part], m_recv.at[way, part], right if way == 0 else left)

    def att_onward(way):
        at = half(way, (here.x + (NX - 1 if way == 0 else 1)) % NX)
        return remote(at, at, n_send.at[way], n_recv.at[way], right if way == 0 else left)

    pairs = ((q_ref, qh_ref), (k_ref, kh_ref), (v_ref, vh_ref))
    order = [(0, SAME_Y), (1, SAME_Y), (0, OTHER_Y), (1, OTHER_Y), (2, SAME_Y), (2, OTHER_Y)]
    queue = Queue((moved, *pairs[a], a, d) for a, ds in order for d in ds)
    each(1, NZ, lambda d: along_z(d).start())
    queue.start(14)
    for a, (src, dst) in enumerate(pairs):
        kept(src, dst, a).start()
    each(1, NZ, lambda d: along_z(d).wait_recv())
    along_y(0, 0).start()
    along_y(1, 0).start()
    on(0)
    for k in range(3):
        for way in range(2):
            along_y(way, k).wait_recv()
            along_y(way, k + 1).start()
            on(1 + 2 * k + way)
            queue.start(3)
    along_y(0, 3).wait_recv()
    along_y(1, 3).wait_recv()
    on(7)

    def next_x(j):
        for way in range(2):
            along_x(way, j).wait_recv()
            if j % 2 == way:
                from_x(way, j).start()
            queue.start(2)
            to_core(3 if way == 0 else 1, j).start()

    for j in range(4):
        next_x(j)

    arrived(*pairs[0], 0)
    arrived(*pairs[1], 1)

    def softmax(step):
        blocks = [step * TOGETHER + i for i in range(TOGETHER)]
        logits = [dot(qh_ref[b], gathered(kh_ref, listed(ids_ref, b)), 1, 1) * SCALE for b in blocks]
        expo = [jnp.exp(x - jnp.max(x, axis=1, keepdims=True)) for x in logits]
        for b, x in zip(blocks, expo):
            probs_ref[b] = x / jnp.sum(x, axis=1, keepdims=True)

    steps = SEQ_LEN // BLOCK // TOGETHER // 4
    for j in range(4):
        each(j * steps, (j + 1) * steps, softmax)
        next_x(4 + j)
    arrived(*pairs[2], 2)

    def attend(chunks):
        blocks = [2 * c + i for c in chunks for i in range(2)]
        out = [dot(probs_ref[b].astype(BF16), gathered(vh_ref, listed(ids_ref, b)), 1, 0) for b in blocks]
        for b, x in zip(blocks, out):
            att_out[block(b), :] = x.astype(BF16)

    def attend_and_send(i):
        attend([seq_at(2 * i + 1), seq_at(2 * i + 2)])
        att(2 * i + 1).start()
        att(2 * i + 2).start()

    each(0, 7, attend_and_send)
    attend([seq_at(15), here.seq])
    att(15).start()
    own_att.start()
    for j in range(8):
        from_x(j % 2, j).wait_recv()
        to_core(2, j).start()
    for y_hi in range(4):
        own_grads(y_hi).start()
        each(1, NX, lambda d: grads(d, y_hi).start())
    for i in (0, 3, 1, 2):
        for j in range(8):
            to_core(i, j).wait_recv()

    def project(head):
        d_out[head] = jnp.dot(g_ref[...], w_all[head % 2, head // 2], preferred_element_type=F32).astype(BF16)

    def project_and_send(d):
        project(seq_at(d))
        d_att(d).start()

    each(1, 16, project_and_send)
    project(here.seq)
    own_d.start()

    def returned(src, dst, a, d):
        to = seq_at(d)
        return remote(
            src.at[rows(to), :], dst.at[:, cols(here.seq)], b_send.at[a, d], b_recv.at[a, d], here.at_seq(to)
        )

    def retained(src, dst, a):
        return pltpu.make_async_copy(src.at[rows(here.seq), :], dst.at[:, cols(here.seq)], own_back.at[a])

    def cleared(step):
        k_sum[block(step), :] = jnp.zeros((BLOCK, HEAD), F32)
        v_sum[block(step), :] = jnp.zeros((BLOCK, HEAD), F32)

    each(0, SEQ_LEN // BLOCK, cleared)

    def add(total, place, terms):
        total[block(place), :] += terms

    def backward(chunks):
        blocks = [2 * c + i for c in chunks for i in range(2)]
        at = [listed(ids_ref, b) for b in blocks]
        d = [dh_ref[block(b), :] for b in blocks]
        probs = [probs_ref[b] for b in blocks]
        d_probs = [dot(x, gathered(vh_ref, i), 1, 1) for x, i in zip(d, at)]
        delta = [jnp.sum(x * y, axis=1, keepdims=True) for x, y in zip(probs, d_probs)]
        d_logits = [(x * (y - z) * SCALE).astype(BF16) for x, y, z in zip(probs, d_probs, delta)]
        dq = [dot(x, gathered(kh_ref, i), 1, 0) for x, i in zip(d_logits, at)]
        for b, x in zip(blocks, dq):
            q_out[block(b), :] = x.astype(BF16)
        dk = [dot(x, qh_ref[b], 0, 0) for x, b in zip(d_logits, blocks)]
        dv = [dot(x.astype(BF16), y, 0, 0) for x, y in zip(probs, d)]
        for total, drawn, terms in ((k_sum, k_drawn, dk), (v_sum, v_drawn, dv)):
            for b, x in zip(blocks, terms):
                for s in range(3):
                    add(total, fixed(b)[s], x[s * BLOCK : (s + 1) * BLOCK])
                for s in range(5, SLOTS):
                    drawn[block((s - 5) * 32 + b), :] = x[s * BLOCK : (s + 1) * BLOCK]
            for s in (3, 4):
                add(total, fixed(0)[s], sum(x[s * BLOCK : (s + 1) * BLOCK] for x in terms))

    def chunk_from(d):
        return (here.seq + 16 - d) % 16

    def backward_and_send(i):
        d_att(2 * i + 1).wait_recv()
        d_att(2 * i + 2).wait_recv()
        backward([chunk_from(2 * i + 1), chunk_from(2 * i + 2)])
        returned(q_out, dq_ref, 0, 15 - 2 * i).start()
        returned(q_out, dq_ref, 0, 14 - 2 * i).start()

    own_att.wait()
    each(1, 16, lambda d: att(d).wait_recv())
    att_copy = pltpu.make_async_copy(mine, att_ref, own_sem.at[5])
    att_copy.start()
    for part in range(2):
        att_x(0, part).start()
        att_x(1, 1 - part).start()
    own_d.wait()
    each(0, 4, backward_and_send)
    for way in range(2):
        att_x(way, way).wait_recv()
        att_onward(way).start()
    each(4, 7, backward_and_send)
    d_att(15).wait_recv()
    backward([chunk_from(15), here.seq])
    returned(q_out, dq_ref, 0, 1).start()
    retained(q_out, dq_ref, 0).start()

    for way in range(2):
        att_x(way, 1 - way).wait_recv()
    for way in range(2):
        att_onward(way).wait_recv()
    for y_hi in range(4):
        own_grads(y_hi).wait()
        each(1, NX, lambda d: grads(d, y_hi).wait_recv())

    def multiply(h):
        a = att4[:, :, cols(h)].reshape(NX * ROWS, HEAD)
        total = lax.dot_general(
            a, g4[...].reshape(NX * ROWS, 4 * HEAD), (((0,), (0,)), ((), ())), preferred_element_type=F32
        )
        product[h] = total
        p_out[h] = total.astype(BF16)

    each(0, HEADS, multiply)

    def half_rows(core):
        return pl.ds(pl.multiple_of(core * 64, 64), 64)

    to_half = remote(
        p_out.at[:, half_rows(1 - here.core), :], p_in, p_send.at[0], p_recv.at[0], here.other_core()
    )
    to_half.start()

    drawn = drawn_ref[...]
    hits = (lax.broadcasted_iota(jnp.int32, (32, 96), 0) == jnp.broadcast_to(drawn, (32, 96))).astype(F32).astype(BF16)
    hits = jnp.concatenate([hits, hits], axis=1)

    def gather_terms(r):
        for total, terms in ((k_sum, k_drawn), (v_sum, v_drawn)):
            x = terms[pl.ds(r, 96, stride=BLOCK), :]
            high = x.astype(BF16)
            low = (x - high.astype(F32)).astype(BF16)
            mine_too = jnp.dot(hits, jnp.concatenate([high, low], axis=0), preferred_element_type=F32)
            at = pl.ds(r, 32, stride=BLOCK)
            total[at, :] = total[at, :] + mine_too

    def gather_some(i):
        for r in range(4):
            gather_terms(4 * i + r)

    each(0, BLOCK // 4, gather_some)
    k_out[...] = k_sum[...].astype(BF16)
    v_out[...] = v_sum[...].astype(BF16)
    order = [(1, SAME_Y), (2, SAME_Y), (1, OTHER_Y), (2, OTHER_Y)]
    results = ((q_out, dq_ref), (k_out, dk_ref), (v_out, dv_ref))
    back = Queue((returned, *results[a], a, d) for a, ds in order for d in ds)
    retained(k_out, dk_ref, 1).start()
    retained(v_out, dv_ref, 2).start()
    to_half.wait()

    def add_core(h):
        total = product[h, half_rows(here.core), :] + p_in[h].astype(F32)
        for y_hi in range(4):
            y_out[y_hi * 2 + h % 2, h // 2] = total[:, y_hi * HEAD : (y_hi + 1) * HEAD].astype(BF16)

    each(0, HEADS, add_core)

    def sum_y(d):
        y = (here.y + d) % NY
        return remote(y_out.at[y], y_in.at[d], s_send.at[d], s_recv.at[d], here.at_y(y))

    each(1, NY, lambda d: sum_y(d).start())
    back.start(30)
    each(1, NY, lambda d: sum_y(d).wait())

    def add_y(z):
        total = y_out[here.y, z].astype(F32)
        for d in range(1, NY):
            total += y_in[d, z].astype(F32)
        z_out[z] = total.astype(BF16)

    each(0, NZ, add_y)

    def sum_z(d):
        z = (here.z + d) % NZ
        return remote(z_out.at[z], z_in.at[d], t_send.at[d], t_recv.at[d], here.at_z(z))

    each(1, NZ, lambda d: sum_z(d).start())
    each(1, NZ, lambda d: sum_z(d).wait())
    total = z_out[here.z].astype(F32)
    for d in range(1, NZ):
        total += z_in[d].astype(F32)
    last_out[...] = total
    swap = remote(last_out, last_in, p_send.at[1], p_recv.at[1], here.other_core())
    swap.start()
    swap.wait()
    first = here.core == 0
    top = jnp.where(first, last_out[...], last_in[...])
    bottom = jnp.where(first, last_in[...], last_out[...])
    gw_ref[:64, :] = jnp.where(first, top[:, :64], top[:, 64:])
    gw_ref[64:, :] = jnp.where(first, bottom[:, :64], bottom[:, 64:])

    for a, (src, dst) in enumerate(results):
        retained(src, dst, a).wait()
        each(1, 16, lambda d: returned(src, dst, a, d).wait())

    for a, (src, dst) in enumerate(pairs):
        each(1, 16, lambda d: moved(src, dst, a, d).wait_send())
    each(1, 16, lambda d: att(d).wait_send())
    each(1, 16, lambda d: d_att(d).wait_send())
    att_copy.wait()
    for y_hi in range(4):
        each(1, NX, lambda d: grads(d, y_hi).wait_send())
    each(1, NZ, lambda d: along_z(d).wait_send())
    for way in range(2):
        for k in range(4):
            along_y(way, k).wait_send()
        for j in range(8):
            along_x(way, j).wait_send()
        for part in range(2):
            att_x(way, part).wait_send()
        att_onward(way).wait_send()
    for j in range(8):
        from_x(j % 2, j).wait_send()
        for i in range(4):
            to_core(i, j).wait_send()


def layer(ids, drawn, q, k, v, g, w):
    any_ = pl.BlockSpec(memory_space=pl.ANY)
    dma = pltpu.SemaphoreType.DMA
    flat = jax.ShapeDtypeStruct((ROWS, WIDTH), BF16)
    by_head, by_block = (SEQ_LEN, HEAD), (SEQ_LEN // BLOCK, BLOCK, HEAD)
    return pl.pallas_call(
        layer_kernel,
        out_shape=(flat,) * 4 + (jax.ShapeDtypeStruct((HEAD, 64), F32),),
        in_specs=[pl.BlockSpec(memory_space=pltpu.SMEM), VMEM] + [any_] * 3 + [VMEM] * 2,
        out_specs=(any_,) * 4 + (VMEM,),
        scratch_shapes=[
            pltpu.VMEM(by_block, BF16),
            pltpu.VMEM(by_block, BF16),
            pltpu.VMEM(by_block, BF16),
            pltpu.VMEM(by_head, BF16),
            pltpu.VMEM((SEQ_LEN // BLOCK, BLOCK, SLOTS * BLOCK), F32),
            pltpu.VMEM((NX, ROWS, WIDTH), BF16),
            pltpu.VMEM((NX, ROWS, 4 * HEAD), BF16),
            pltpu.VMEM((2, NZ, WIDTH, HEAD), BF16),
            pltpu.VMEM(by_head, BF16),
            pltpu.VMEM((HEADS, ROWS, HEAD), BF16),
            pltpu.VMEM(by_head, BF16),
            pltpu.VMEM(by_head, BF16),
            pltpu.VMEM(by_head, BF16),
            pltpu.VMEM(by_head, F32),
            pltpu.VMEM(by_head, F32),
            pltpu.VMEM((96 * BLOCK, HEAD), F32),
            pltpu.VMEM((96 * BLOCK, HEAD), F32),
            pltpu.VMEM((HEADS, HEAD, 4 * HEAD), F32),
            pltpu.VMEM((HEADS, HEAD, 4 * HEAD), BF16),
            pltpu.VMEM((HEADS, 64, 4 * HEAD), BF16),
            pltpu.VMEM((NY, NZ, 64, HEAD), BF16),
            pltpu.VMEM((NY, NZ, 64, HEAD), BF16),
            pltpu.VMEM((NZ, 64, HEAD), BF16),
            pltpu.VMEM((NZ, 64, HEAD), BF16),
            pltpu.VMEM((64, HEAD), F32),
            pltpu.VMEM((64, HEAD), F32),
            dma((5, 16)), dma((5, 16)), dma((6,)), dma((NZ,)), dma((NZ,)), dma((2, 4)), dma((2, 4)),
            dma((2, 8)), dma((2, 8)), dma((8,)), dma((8,)), dma((4, 8)), dma((4, 8)),
            dma((4, 4)), dma((4, 4)), dma((2, 2)), dma((2, 2)), dma((2,)), dma((2,)),
            dma((3, 16)), dma((3, 16)), dma((3,)), dma((2,)), dma((2,)),
            dma((NY,)), dma((NY,)), dma((NZ,)), dma((NZ,)),
        ],
        compiler_params=pltpu.CompilerParams(
            collective_id=0, has_side_effects=True, vmem_limit_bytes=50 * 2**20
        ),
        name="layer",
    )(ids, drawn, q, k, v, g, w)


def in_blocks(flat):
    return flat.reshape(ROWS // BLOCK, BLOCK, WIDTH)


def local(query_rows, key_rows, value_rows, out_weight, grad_out, block_list):
    ids = block_list[0]
    drawn = ids[:, 5:].T.reshape(1, 96)
    att, dq, dk, dv, grad_weight = layer(
        ids, drawn, in_blocks(query_rows), in_blocks(key_rows), in_blocks(value_rows), grad_out[0], out_weight
    )
    return (att[None], dq[None], dk[None], dv[None], grad_weight)


def solution(mesh):
    return jax.shard_map(
        local,
        mesh=mesh,
        in_specs=(
            P("dp", "seq", None),
            P("dp", "seq", None),
            P("dp", "seq", None),
            P("seq", "dp"),
            P("dp", "seq", None),
            P("dp", None, None),
        ),
        out_specs=(
            P("dp", "seq", None),
            P("dp", "seq", None),
            P("dp", "seq", None),
            P("dp", "seq", None),
            P("seq", "dp"),
        ),
        check_vma=False,
    )
```

```python
import functools
import math

import jax
import jax.numpy as jnp
from jax import lax
from jax.experimental import pallas as pl
from jax.experimental.pallas import tpu as pltpu
from jax.sharding import PartitionSpec as P

MESH = pl.DeviceIdType.MESH
F32, BF16 = jnp.float32, jnp.bfloat16
SEQ_LEN, HEADS, HEAD, BLOCK, WIDTH = 2048, 16, 128, 64, 2048
ROWS = SEQ_LEN // 16
NX, NY, NZ = 4, 8, 8
OFFSETS = (0, -1, 1, -2, 2, -3, 3, 4)


SAME_Y, OTHER_Y = (8, 6, 10, 4, 12, 2, 14), (7, 9, 5, 11, 3, 13, 1, 15)


class Queue:
    def __init__(self, copies):
        self.copies = list(copies)

    def start(self, count):
        for make, *args in self.copies[:count]:
            make(*args).start()
        self.copies = self.copies[count:]


class Place:
    def __init__(self):
        self.dp = lax.axis_index("dp")
        self.seq = lax.axis_index("seq")
        self.y_hi = self.dp // 8
        self.x = (self.dp // 2) % 4
        self.core = self.dp % 2
        self.z = self.seq // 2
        self.y_lo = self.seq % 2
        self.y = 2 * self.y_hi + self.y_lo

    def dp_of(self, y_hi=None, x=None, core=None):
        y_hi = self.y_hi if y_hi is None else y_hi
        x = self.x if x is None else x
        core = self.core if core is None else core
        return y_hi * 8 + x * 2 + core

    def at_x(self, x):
        return (self.dp_of(x=x), self.seq)

    def at_y(self, y):
        return (self.dp_of(y_hi=y // 2), 2 * self.z + y % 2)

    def at_z(self, z):
        return (self.dp, 2 * z + self.y_lo)

    def at_seq(self, seq):
        return (self.dp, seq)

    def other_core(self):
        return (self.dp_of(core=1 - self.core), self.seq)


def greet(barrier, place, others):
    def one(d, _):
        to = place.at_seq((place.seq + d) % 16)
        pl.semaphore_signal(barrier, inc=1, device_id=to, device_id_type=MESH)
        return 0

    lax.fori_loop(1, 16, one, 0)
    for to in others:
        pl.semaphore_signal(barrier, inc=1, device_id=to, device_id_type=MESH)
    pl.semaphore_wait(barrier, 15 + len(others))


def remote(src, dst, send, recv, to):
    return pltpu.make_async_remote_copy(
        src_ref=src, dst_ref=dst, send_sem=send, recv_sem=recv, device_id=to, device_id_type=MESH
    )


def each(low, high, act):
    def one(i, _):
        act(i)
        return 0

    lax.fori_loop(low, high, one, 0)


def cols(i):
    return pl.ds(pl.multiple_of(i * HEAD, HEAD), HEAD)


def rows(i):
    return pl.ds(pl.multiple_of(i * ROWS, ROWS), ROWS)


def dot(a, b, i, j):
    return lax.dot_general(a, b, (((i,), (j,)), ((), ())), preferred_element_type=F32)


def block(b):
    return pl.ds(pl.multiple_of(b * BLOCK, BLOCK), BLOCK)


SLOTS = 8
SCALE = 1.0 / math.sqrt(HEAD)
TOGETHER = 4


def fixed(b):
    return [(b + 31) % 32, b, (b + 1) % 32, 0, 31]


def listed(ids_ref, b):
    return fixed(b) + [ids_ref[b, s] for s in range(5, SLOTS)]


def gathered(ref, at):
    return jnp.concatenate([ref[i] for i in at], axis=0)


VMEM = pl.BlockSpec(memory_space=pltpu.VMEM)


def layer_kernel(
    ids_ref, drawn_ref, q_ref, k_ref, v_ref, g_ref, w_ref, att_ref, dq_ref, dk_ref, dv_ref, gw_ref,
    qh_ref, kh_ref, vh_ref, dh_ref, probs_ref, mine, att4, g4, w_all, att_out, d_out, q_out, k_out, v_out,
    k_sum, v_sum, k_drawn, v_drawn, product, p_out, p_in, y_out, y_in, z_out, z_in, last_out, last_in,
    a_send, a_recv, own_sem, z_send, z_recv, y_send, y_recv, x_send, x_recv,
    f_send, f_recv, c_send, c_recv, g_send, g_recv, m_send, m_recv, n_send, n_recv,
    b_send, b_recv, own_back, p_send, p_recv, s_send, s_recv, t_send, t_recv,
):
    here = Place()
    up = here.at_y((here.y + 1) % NY)
    down = here.at_y((here.y + NY - 1) % NY)
    right = here.at_x((here.x + 1) % NX)
    left = here.at_x((here.x + NX - 1) % NX)
    others = [here.other_core()] + [here.at_x((here.x + d) % NX) for d in range(1, NX)]
    for d in range(1, 4):
        for y_lo in range(2):
            others.append((here.dp_of(y_hi=(here.y_hi + d) % 4), 2 * here.z + y_lo))
    for core in range(2):
        others.append((here.dp_of(x=here.z % 4, core=core), 2 * (2 * here.x + 1 - here.z // 4) + here.y_lo))
        others.append((here.dp_of(x=here.z // 2, core=core), 2 * ((1 - here.z % 2) * 4 + here.x) + here.y_lo))
    greet(pltpu.get_barrier_semaphore(), here, others)

    def seq_at(d):
        return (here.seq + d) % 16

    def moved(src, dst, a, d):
        return remote(
            src.at[:, :, cols(seq_at(d))], dst.at[pl.ds(2 * here.seq, 2)], a_send.at[a, d], a_recv.at[a, d],
            here.at_seq(seq_at(d)),
        )

    def kept(src, dst, a):
        return pltpu.make_async_copy(src.at[:, :, cols(here.seq)], dst.at[pl.ds(2 * here.seq, 2)], own_sem.at[a])

    def arrived(src, dst, a):
        kept(src, dst, a).wait()
        each(1, 16, lambda d: moved(src, dst, a, d).wait_recv())

    def weights(y, x=None, z=slice(None)):
        at = pl.multiple_of(here.dp_of(y // 2, x) * 64, 64)
        return w_all.at[y % 2, z, pl.ds(at, 64), :]

    own = w_all.at[here.y_lo, here.z, pl.ds(pl.multiple_of(here.dp * 64, 64), 64), :]
    own[...] = w_ref[...].astype(F32).T.astype(BF16)

    def along_z(d):
        return remote(own, own, z_send.at[d], z_recv.at[d], here.at_z((here.z + d) % NZ))

    def along_y(way, k):
        sign = 1 if way == 0 else -1
        part = slice(None) if k < 3 else (pl.ds(0, 4) if way == 0 else pl.ds(4, 4))
        at = weights((here.y - sign * k + NY) % NY, z=part)
        return remote(at, at, y_send.at[way, k], y_recv.at[way, k], up if way == 0 else down)

    def along_x(way, j):
        at = weights((here.y + OFFSETS[j] + NY) % NY)
        return remote(at, at, x_send.at[way, j], x_recv.at[way, j], right if way == 0 else left)

    def from_x(way, j):
        x = (here.x + (NX - 1 if way == 0 else 1)) % NX
        at = weights((here.y + OFFSETS[j] + NY) % NY, x)
        return remote(at, at, f_send.at[j], f_recv.at[j], right if way == 0 else left)

    def to_core(i, j):
        at = weights((here.y + OFFSETS[j] + NY) % NY, (here.x + i) % NX)
        return remote(at, at, c_send.at[i, j], c_recv.at[i, j], here.other_core())

    def on(j):
        along_x(0, j).start()
        along_x(1, j).start()
        to_core(0, j).start()

    def grads(d):
        return remote(g_ref, g4.at[here.x], g_send.at[d], g_recv.at[d], here.at_x((here.x + d) % NX))

    own_grads = pltpu.make_async_copy(g_ref, g4.at[here.x], g_send.at[0])

    def att(d):
        to = seq_at(d)
        return remote(
            att_out.at[rows(to), :], mine.at[:, cols(here.seq)], a_send.at[3, d], a_recv.at[3, d], here.at_seq(to)
        )

    own_att = pltpu.make_async_copy(att_out.at[rows(here.seq), :], mine.at[:, cols(here.seq)], own_sem.at[3])

    def d_att(d):
        to = seq_at(d)
        return remote(d_out.at[to], dh_ref.at[rows(here.seq), :], a_send.at[4, d], a_recv.at[4, d], here.at_seq(to))

    own_d = pltpu.make_async_copy(d_out.at[here.seq], dh_ref.at[rows(here.seq), :], own_sem.at[4])

    def quarter(x):
        return mine.at[:, pl.ds(pl.multiple_of(x * 4 * HEAD, 4 * HEAD), 4 * HEAD)]

    def att_x(d):
        x = (here.x + d) % NX
        return remote(quarter(x), att4.at[here.x], m_send.at[d], m_recv.at[d], here.at_x(x))

    own_att_x = pltpu.make_async_copy(quarter(here.x), att4.at[here.x], m_send.at[0])

    pairs = ((q_ref, qh_ref), (k_ref, kh_ref), (v_ref, vh_ref))
    order = [(0, SAME_Y), (1, SAME_Y), (0, OTHER_Y), (1, OTHER_Y), (2, SAME_Y), (2, OTHER_Y)]
    queue = Queue((moved, *pairs[a], a, d) for a, ds in order for d in ds)
    each(1, NZ, lambda d: along_z(d).start())
    queue.start(14)
    for a, (src, dst) in enumerate(pairs):
        kept(src, dst, a).start()
    each(1, NZ, lambda d: along_z(d).wait_recv())
    along_y(0, 0).start()
    along_y(1, 0).start()
    on(0)
    for k in range(3):
        for way in range(2):
            along_y(way, k).wait_recv()
            along_y(way, k + 1).start()
            on(1 + 2 * k + way)
            queue.start(3)
    along_y(0, 3).wait_recv()
    along_y(1, 3).wait_recv()
    on(7)

    def next_x(j):
        for way in range(2):
            along_x(way, j).wait_recv()
            if j % 2 == way:
                from_x(way, j).start()
            queue.start(2)
            to_core(3 if way == 0 else 1, j).start()

    for j in range(4):
        next_x(j)

    arrived(*pairs[0], 0)
    arrived(*pairs[1], 1)

    def softmax(step):
        blocks = [step * TOGETHER + i for i in range(TOGETHER)]
        logits = [dot(qh_ref[b], gathered(kh_ref, listed(ids_ref, b)), 1, 1) * SCALE for b in blocks]
        expo = [jnp.exp(x - jnp.max(x, axis=1, keepdims=True)) for x in logits]
        for b, x in zip(blocks, expo):
            probs_ref[b] = x / jnp.sum(x, axis=1, keepdims=True)

    steps = SEQ_LEN // BLOCK // TOGETHER // 4
    for j in range(4):
        each(j * steps, (j + 1) * steps, softmax)
        next_x(4 + j)
    arrived(*pairs[2], 2)

    def attend(chunks):
        blocks = [2 * c + i for c in chunks for i in range(2)]
        out = [dot(probs_ref[b].astype(BF16), gathered(vh_ref, listed(ids_ref, b)), 1, 0) for b in blocks]
        for b, x in zip(blocks, out):
            att_out[block(b), :] = x.astype(BF16)

    def attend_and_send(i):
        attend([seq_at(2 * i + 1), seq_at(2 * i + 2)])
        att(2 * i + 1).start()
        att(2 * i + 2).start()

    each(0, 7, attend_and_send)
    attend([seq_at(15), here.seq])
    att(15).start()
    own_att.start()
    for j in range(8):
        from_x(j % 2, j).wait_recv()
        to_core(2, j).start()
    own_grads.start()
    each(1, NX, lambda d: grads(d).start())
    for i in (0, 3, 1, 2):
        for j in range(8):
            to_core(i, j).wait_recv()

    def project(head):
        d_out[head] = jnp.dot(g_ref[...], w_all[head % 2, head // 2], preferred_element_type=F32).astype(BF16)

    def project_and_send(d):
        project(seq_at(d))
        d_att(d).start()

    each(1, 16, project_and_send)
    project(here.seq)
    own_d.start()

    def returned(src, dst, a, d):
        to = seq_at(d)
        return remote(
            src.at[rows(to), :], dst.at[:, cols(here.seq)], b_send.at[a, d], b_recv.at[a, d], here.at_seq(to)
        )

    def retained(src, dst, a):
        return pltpu.make_async_copy(src.at[rows(here.seq), :], dst.at[:, cols(here.seq)], own_back.at[a])

    def cleared(step):
        k_sum[block(step), :] = jnp.zeros((BLOCK, HEAD), F32)
        v_sum[block(step), :] = jnp.zeros((BLOCK, HEAD), F32)

    each(0, SEQ_LEN // BLOCK, cleared)

    def add(total, place, terms):
        total[block(place), :] += terms

    def backward(chunks):
        blocks = [2 * c + i for c in chunks for i in range(2)]
        at = [listed(ids_ref, b) for b in blocks]
        d = [dh_ref[block(b), :] for b in blocks]
        probs = [probs_ref[b] for b in blocks]
        d_probs = [dot(x, gathered(vh_ref, i), 1, 1) for x, i in zip(d, at)]
        delta = [jnp.sum(x * y, axis=1, keepdims=True) for x, y in zip(probs, d_probs)]
        d_logits = [(x * (y - z) * SCALE).astype(BF16) for x, y, z in zip(probs, d_probs, delta)]
        dq = [dot(x, gathered(kh_ref, i), 1, 0) for x, i in zip(d_logits, at)]
        for b, x in zip(blocks, dq):
            q_out[block(b), :] = x.astype(BF16)
        dk = [dot(x, qh_ref[b], 0, 0) for x, b in zip(d_logits, blocks)]
        dv = [dot(x.astype(BF16), y, 0, 0) for x, y in zip(probs, d)]
        for total, drawn, terms in ((k_sum, k_drawn, dk), (v_sum, v_drawn, dv)):
            for b, x in zip(blocks, terms):
                for s in range(3):
                    add(total, fixed(b)[s], x[s * BLOCK : (s + 1) * BLOCK])
                for s in range(5, SLOTS):
                    drawn[block((s - 5) * 32 + b), :] = x[s * BLOCK : (s + 1) * BLOCK]
            for s in (3, 4):
                add(total, fixed(0)[s], sum(x[s * BLOCK : (s + 1) * BLOCK] for x in terms))

    def chunk_from(d):
        return (here.seq + 16 - d) % 16

    def backward_and_send(i):
        d_att(2 * i + 1).wait_recv()
        d_att(2 * i + 2).wait_recv()
        backward([chunk_from(2 * i + 1), chunk_from(2 * i + 2)])
        returned(q_out, dq_ref, 0, 15 - 2 * i).start()
        returned(q_out, dq_ref, 0, 14 - 2 * i).start()

    own_att.wait()
    each(1, 16, lambda d: att(d).wait_recv())
    att_copy = pltpu.make_async_copy(mine, att_ref, own_sem.at[5])
    att_copy.start()
    own_att_x.start()
    each(1, NX, lambda d: att_x(d).start())
    own_d.wait()
    each(0, 7, backward_and_send)
    d_att(15).wait_recv()
    backward([chunk_from(15), here.seq])
    returned(q_out, dq_ref, 0, 1).start()
    retained(q_out, dq_ref, 0).start()

    drawn = drawn_ref[...]
    hits = (lax.broadcasted_iota(jnp.int32, (32, 96), 0) == jnp.broadcast_to(drawn, (32, 96))).astype(F32).astype(BF16)
    hits = jnp.concatenate([hits, hits], axis=1)

    def gather_terms(r):
        for total, terms in ((k_sum, k_drawn), (v_sum, v_drawn)):
            x = terms[pl.ds(r, 96, stride=BLOCK), :]
            high = x.astype(BF16)
            low = (x - high.astype(F32)).astype(BF16)
            mine_too = jnp.dot(hits, jnp.concatenate([high, low], axis=0), preferred_element_type=F32)
            at = pl.ds(r, 32, stride=BLOCK)
            total[at, :] = total[at, :] + mine_too

    def gather_some(i):
        for r in range(4):
            gather_terms(4 * i + r)

    each(0, BLOCK // 4, gather_some)
    k_out[...] = k_sum[...].astype(BF16)
    v_out[...] = v_sum[...].astype(BF16)
    order = [(1, SAME_Y), (2, SAME_Y), (1, OTHER_Y), (2, OTHER_Y)]
    results = ((q_out, dq_ref), (k_out, dk_ref), (v_out, dv_ref))
    back = Queue((returned, *results[a], a, d) for a, ds in order for d in ds)
    retained(k_out, dk_ref, 1).start()
    retained(v_out, dv_ref, 2).start()
    back.start(14)

    own_att_x.wait()
    own_grads.wait()
    each(1, NX, lambda d: att_x(d).wait_recv())
    each(1, NX, lambda d: grads(d).wait_recv())

    def multiply(i):
        head, y_hi = i // 4, i % 4
        a = att4[:, :, cols(head)].reshape(NX * ROWS, HEAD)
        g = g4[:, :, pl.ds(pl.multiple_of(y_hi * 4 * HEAD, 4 * HEAD), 4 * HEAD)].reshape(NX * ROWS, 4 * HEAD)
        total = dot(a, g, 0, 0)
        product[i] = total
        p_out[i] = total.astype(BF16)

    each(0, HEADS, multiply)

    def half_rows(core):
        return pl.ds(pl.multiple_of(core * 64, 64), 64)

    to_half = remote(
        p_out.at[:, half_rows(1 - here.core), :], p_in, p_send.at[0], p_recv.at[0], here.other_core()
    )
    to_half.start()

    to_half.wait()

    def add_core(i):
        head, y_hi = i // 4, i % 4
        total = product[i, half_rows(here.core), :] + p_in[i].astype(F32)
        for x in range(NX):
            slot = (1 - head // 2) * 4 + x
            y_out[2 * y_hi + head % 2, slot] = total[:, x * HEAD : (x + 1) * HEAD].astype(BF16)

    each(0, HEADS, add_core)

    def half_of(k, way):
        return slice(None) if k > 0 else pl.ds(4 * way, 4)

    def target(way, k):
        return (here.y + (4 - k if way == 0 else 4 + k)) % NY

    def sum_y(way, k):
        part = half_of(k, way)
        return remote(
            y_out.at[target(way, k), part], y_in.at[4 * way + k, part], s_send.at[way, k], s_recv.at[way, k],
            up if way == 0 else down,
        )

    def next_y(k):
        for way in range(2):
            sum_y(way, k - 1).wait_recv()
            low = 0 if k > 1 else 4 * way

            def add_y(slot):
                mine_too = y_out[target(way, k), slot].astype(F32)
                y_out[target(way, k), slot] = (mine_too + y_in[4 * way + k - 1, slot].astype(F32)).astype(BF16)

            each(low, NZ if k > 1 else low + 4, add_y)
            sum_y(way, k).start()

    sum_y(0, 0).start()
    sum_y(1, 0).start()

    next_y(1)
    back.start(5)
    next_y(2)
    back.start(5)
    next_y(3)
    back.start(6)
    sum_y(0, 3).wait_recv()
    sum_y(1, 3).wait_recv()

    def finish_y(z):
        total = y_out[here.y, z].astype(F32) + y_in[3, z].astype(F32) + y_in[7, z].astype(F32)
        z_out[z] = total.astype(BF16)

    each(0, NZ, finish_y)

    def sum_z(d):
        z = (here.z + d) % NZ
        return remote(z_out.at[z], z_in.at[d], t_send.at[d], t_recv.at[d], here.at_z(z))

    each(1, NZ, lambda d: sum_z(d).start())
    each(1, NZ, lambda d: sum_z(d).wait())
    total = z_out[here.z].astype(F32)
    for d in range(1, NZ):
        total += z_in[d].astype(F32)
    last_out[...] = total

    def to_owner(core):
        to = (here.dp_of(x=here.z % 4, core=core), 2 * (2 * here.x + 1 - here.z // 4) + here.y_lo)
        return remote(last_out, last_in.at[here.core], n_send.at[core], n_recv.at[here.core], to)

    def from_owner(core):
        to = (here.dp_of(x=here.z % 4, core=core), 2 * (2 * here.x + 1 - here.z // 4) + here.y_lo)
        return remote(last_out, last_in.at[core], n_send.at[core], n_recv.at[core], to)

    for core in range(2):
        to_owner(core).start()
    for core in range(2):
        from_owner(core).wait_recv()
    first = here.core == 0
    top, bottom = last_in[0], last_in[1]
    gw_ref[:64, :] = jnp.where(first, top[:, :64], top[:, 64:])
    gw_ref[64:, :] = jnp.where(first, bottom[:, :64], bottom[:, 64:])

    for a, (src, dst) in enumerate(results):
        retained(src, dst, a).wait()
        each(1, 16, lambda d: returned(src, dst, a, d).wait())

    for a, (src, dst) in enumerate(pairs):
        each(1, 16, lambda d: moved(src, dst, a, d).wait_send())
    each(1, 16, lambda d: att(d).wait_send())
    each(1, 16, lambda d: d_att(d).wait_send())
    att_copy.wait()
    each(1, NX, lambda d: grads(d).wait_send())
    each(1, NX, lambda d: att_x(d).wait_send())
    for core in range(2):
        to_owner(core).wait_send()
    for way in range(2):
        for k in range(4):
            sum_y(way, k).wait_send()
    each(1, NZ, lambda d: along_z(d).wait_send())
    for way in range(2):
        for k in range(4):
            along_y(way, k).wait_send()
        for j in range(8):
            along_x(way, j).wait_send()
    for j in range(8):
        from_x(j % 2, j).wait_send()
        for i in range(4):
            to_core(i, j).wait_send()


def layer(ids, drawn, q, k, v, g, w):
    any_ = pl.BlockSpec(memory_space=pl.ANY)
    dma = pltpu.SemaphoreType.DMA
    flat = jax.ShapeDtypeStruct((ROWS, WIDTH), BF16)
    by_head, by_block = (SEQ_LEN, HEAD), (SEQ_LEN // BLOCK, BLOCK, HEAD)
    return pl.pallas_call(
        layer_kernel,
        out_shape=(flat,) * 4 + (jax.ShapeDtypeStruct((HEAD, 64), F32),),
        in_specs=[pl.BlockSpec(memory_space=pltpu.SMEM), VMEM] + [pl.BlockSpec(memory_space=pltpu.HBM)] * 3 + [VMEM] * 2,
        out_specs=(any_,) * 4 + (VMEM,),
        scratch_shapes=[
            pltpu.VMEM(by_block, BF16),
            pltpu.VMEM(by_block, BF16),
            pltpu.VMEM(by_block, BF16),
            pltpu.VMEM(by_head, BF16),
            pltpu.VMEM((SEQ_LEN // BLOCK, BLOCK, SLOTS * BLOCK), F32),
            pltpu.VMEM((ROWS, WIDTH), BF16),
            pltpu.VMEM((NX, ROWS, 4 * HEAD), BF16),
            pltpu.VMEM((NX, ROWS, WIDTH), BF16),
            pltpu.VMEM((2, NZ, WIDTH, HEAD), BF16),
            pltpu.VMEM(by_head, BF16),
            pltpu.VMEM((HEADS, ROWS, HEAD), BF16),
            pltpu.VMEM(by_head, BF16),
            pltpu.VMEM(by_head, BF16),
            pltpu.VMEM(by_head, BF16),
            pltpu.VMEM(by_head, F32),
            pltpu.VMEM(by_head, F32),
            pltpu.VMEM((96 * BLOCK, HEAD), F32),
            pltpu.VMEM((96 * BLOCK, HEAD), F32),
            pltpu.VMEM((HEADS, HEAD, 4 * HEAD), F32),
            pltpu.VMEM((HEADS, HEAD, 4 * HEAD), BF16),
            pltpu.VMEM((HEADS, 64, 4 * HEAD), BF16),
            pltpu.VMEM((NY, NZ, 64, HEAD), BF16),
            pltpu.VMEM((NY, NZ, 64, HEAD), BF16),
            pltpu.VMEM((NZ, 64, HEAD), BF16),
            pltpu.VMEM((NZ, 64, HEAD), BF16),
            pltpu.VMEM((64, HEAD), F32),
            pltpu.VMEM((2, 64, HEAD), F32),
            dma((5, 16)), dma((5, 16)), dma((6,)), dma((NZ,)), dma((NZ,)), dma((2, 4)), dma((2, 4)),
            dma((2, 8)), dma((2, 8)), dma((8,)), dma((8,)), dma((4, 8)), dma((4, 8)),
            dma((4,)), dma((4,)), dma((4,)), dma((4,)), dma((2,)), dma((2,)),
            dma((3, 16)), dma((3, 16)), dma((3,)), dma((1,)), dma((1,)),
            dma((2, 4)), dma((2, 4)), dma((NZ,)), dma((NZ,)),
        ],
        compiler_params=pltpu.CompilerParams(
            collective_id=0, has_side_effects=True, vmem_limit_bytes=50 * 2**20
        ),
        name="layer",
    )(ids, drawn, q, k, v, g, w)


def in_blocks(flat):
    return flat.reshape(ROWS // BLOCK, BLOCK, WIDTH)


def local(query_rows, key_rows, value_rows, out_weight, grad_out, block_list):
    ids = block_list[0]
    drawn = ids[:, 5:].T.reshape(1, 96)
    att, dq, dk, dv, grad_weight = layer(
        ids, drawn, in_blocks(query_rows), in_blocks(key_rows), in_blocks(value_rows), grad_out[0], out_weight
    )
    return (att[None], dq[None], dk[None], dv[None], grad_weight)


def solution(mesh):
    return jax.shard_map(
        local,
        mesh=mesh,
        in_specs=(
            P("dp", "seq", None),
            P("dp", "seq", None),
            P("dp", "seq", None),
            P("seq", "dp"),
            P("dp", "seq", None),
            P("dp", None, None),
        ),
        out_specs=(
            P("dp", "seq", None),
            P("dp", "seq", None),
            P("dp", "seq", None),
            P("dp", "seq", None),
            P("seq", "dp"),
        ),
        check_vma=False,
    )
```

```python
import functools
import math

import jax
import jax.numpy as jnp
from jax import lax
from jax.experimental import pallas as pl
from jax.experimental.pallas import tpu as pltpu
from jax.sharding import PartitionSpec as P

MESH = pl.DeviceIdType.MESH
F32, BF16 = jnp.float32, jnp.bfloat16
SEQ_LEN, HEADS, HEAD, BLOCK, WIDTH = 2048, 16, 128, 64, 2048
ROWS = SEQ_LEN // 16
NX, NY, NZ = 4, 8, 8
OFFSETS = (0, -1, 1, -2, 2, -3, 3, 4)


SAME_Y, OTHER_Y = (8, 6, 10, 4, 12, 2, 14), (7, 9, 5, 11, 3, 13, 1, 15)


class Queue:
    def __init__(self, copies):
        self.copies = list(copies)

    def start(self, count):
        for make, *args in self.copies[:count]:
            make(*args).start()
        self.copies = self.copies[count:]


class Place:
    def __init__(self):
        self.dp = lax.axis_index("dp")
        self.seq = lax.axis_index("seq")
        self.y_hi = self.dp // 8
        self.x = (self.dp // 2) % 4
        self.core = self.dp % 2
        self.z = self.seq // 2
        self.y_lo = self.seq % 2
        self.y = 2 * self.y_hi + self.y_lo

    def dp_of(self, y_hi=None, x=None, core=None):
        y_hi = self.y_hi if y_hi is None else y_hi
        x = self.x if x is None else x
        core = self.core if core is None else core
        return y_hi * 8 + x * 2 + core

    def at_x(self, x):
        return (self.dp_of(x=x), self.seq)

    def at_y(self, y):
        return (self.dp_of(y_hi=y // 2), 2 * self.z + y % 2)

    def at_z(self, z):
        return (self.dp, 2 * z + self.y_lo)

    def at_seq(self, seq):
        return (self.dp, seq)

    def other_core(self):
        return (self.dp_of(core=1 - self.core), self.seq)


def greet(barrier, place, others):
    def one(d, _):
        to = place.at_seq((place.seq + d) % 16)
        pl.semaphore_signal(barrier, inc=1, device_id=to, device_id_type=MESH)
        return 0

    lax.fori_loop(1, 16, one, 0)
    for to in others:
        pl.semaphore_signal(barrier, inc=1, device_id=to, device_id_type=MESH)
    pl.semaphore_wait(barrier, 15 + len(others))


def remote(src, dst, send, recv, to):
    return pltpu.make_async_remote_copy(
        src_ref=src, dst_ref=dst, send_sem=send, recv_sem=recv, device_id=to, device_id_type=MESH
    )


def each(low, high, act):
    def one(i, _):
        act(i)
        return 0

    lax.fori_loop(low, high, one, 0)


def cols(i):
    return pl.ds(pl.multiple_of(i * HEAD, HEAD), HEAD)


def rows(i):
    return pl.ds(pl.multiple_of(i * ROWS, ROWS), ROWS)


def dot(a, b, i, j):
    return lax.dot_general(a, b, (((i,), (j,)), ((), ())), preferred_element_type=F32)


def block(b):
    return pl.ds(pl.multiple_of(b * BLOCK, BLOCK), BLOCK)


SLOTS = 8
SCALE = 1.0 / math.sqrt(HEAD)
TOGETHER = 4


def fixed(b):
    return [(b + 31) % 32, b, (b + 1) % 32, 0, 31]


def listed(ids_ref, b):
    return fixed(b) + [ids_ref[b, s] for s in range(5, SLOTS)]


def gathered(ref, at):
    return jnp.concatenate([ref[i] for i in at], axis=0)


VMEM = pl.BlockSpec(memory_space=pltpu.VMEM)


def layer_kernel(
    ids_ref, drawn_ref, q_ref, k_ref, v_ref, g_ref, w_ref, att_ref, dq_ref, dk_ref, dv_ref, gw_ref,
    qh_ref, kh_ref, vh_ref, dh_ref, probs_ref, mine, att4, g4, w_all, att_out, d_out, q_out, k_out, v_out,
    k_sum, v_sum, k_drawn, v_drawn, product, p_out, p_in, y_out, y_in, z_out, z_in, last_out, last_in,
    a_send, a_recv, own_sem, z_send, z_recv, y_send, y_recv, x_send, x_recv,
    f_send, f_recv, c_send, c_recv, g_send, g_recv, m_send, m_recv, n_send, n_recv,
    b_send, b_recv, own_back, p_send, p_recv, s_send, s_recv, t_send, t_recv,
):
    here = Place()
    up = here.at_y((here.y + 1) % NY)
    down = here.at_y((here.y + NY - 1) % NY)
    right = here.at_x((here.x + 1) % NX)
    left = here.at_x((here.x + NX - 1) % NX)
    others = [here.other_core()] + [here.at_x((here.x + d) % NX) for d in range(1, NX)]
    for d in range(1, 4):
        for y_lo in range(2):
            others.append((here.dp_of(y_hi=(here.y_hi + d) % 4), 2 * here.z + y_lo))
    for core in range(2):
        others.append((here.dp_of(x=here.z % 4, core=core), 2 * (2 * here.x + 1 - here.z // 4) + here.y_lo))
        others.append((here.dp_of(x=here.z // 2, core=core), 2 * ((1 - here.z % 2) * 4 + here.x) + here.y_lo))
    greet(pltpu.get_barrier_semaphore(), here, others)

    def seq_at(d):
        return (here.seq + d) % 16

    def moved(src, dst, a, d):
        return remote(
            src.at[:, :, cols(seq_at(d))], dst.at[pl.ds(2 * here.seq, 2)], a_send.at[a, d], a_recv.at[a, d],
            here.at_seq(seq_at(d)),
        )

    def kept(src, dst, a):
        return pltpu.make_async_copy(src.at[:, :, cols(here.seq)], dst.at[pl.ds(2 * here.seq, 2)], own_sem.at[a])

    def arrived(src, dst, a):
        kept(src, dst, a).wait()
        each(1, 16, lambda d: moved(src, dst, a, d).wait_recv())

    def weights(y, x=None, z=slice(None)):
        at = pl.multiple_of(here.dp_of(y // 2, x) * 64, 64)
        return w_all.at[y % 2, z, pl.ds(at, 64), :]

    own = w_all.at[here.y_lo, here.z, pl.ds(pl.multiple_of(here.dp * 64, 64), 64), :]
    own[...] = w_ref[...].astype(F32).T.astype(BF16)

    def along_z(d):
        return remote(own, own, z_send.at[d], z_recv.at[d], here.at_z((here.z + d) % NZ))

    def along_y(way, k):
        sign = 1 if way == 0 else -1
        part = slice(None) if k < 3 else (pl.ds(0, 4) if way == 0 else pl.ds(4, 4))
        at = weights((here.y - sign * k + NY) % NY, z=part)
        return remote(at, at, y_send.at[way, k], y_recv.at[way, k], up if way == 0 else down)

    def along_x(way, j):
        at = weights((here.y + OFFSETS[j] + NY) % NY)
        return remote(at, at, x_send.at[way, j], x_recv.at[way, j], right if way == 0 else left)

    def from_x(way, j):
        x = (here.x + (NX - 1 if way == 0 else 1)) % NX
        at = weights((here.y + OFFSETS[j] + NY) % NY, x)
        return remote(at, at, f_send.at[j], f_recv.at[j], right if way == 0 else left)

    def to_core(i, j):
        at = weights((here.y + OFFSETS[j] + NY) % NY, (here.x + i) % NX)
        return remote(at, at, c_send.at[i, j], c_recv.at[i, j], here.other_core())

    def on(j):
        along_x(0, j).start()
        along_x(1, j).start()
        to_core(0, j).start()

    def grads(d):
        return remote(g_ref, g4.at[here.x], g_send.at[d], g_recv.at[d], here.at_x((here.x + d) % NX))

    own_grads = pltpu.make_async_copy(g_ref, g4.at[here.x], g_send.at[0])

    def att(d):
        to = seq_at(d)
        return remote(
            att_out.at[rows(to), :], mine.at[:, cols(here.seq)], a_send.at[3, d], a_recv.at[3, d], here.at_seq(to)
        )

    own_att = pltpu.make_async_copy(att_out.at[rows(here.seq), :], mine.at[:, cols(here.seq)], own_sem.at[3])

    def d_att(d):
        to = seq_at(d)
        return remote(d_out.at[to], dh_ref.at[rows(here.seq), :], a_send.at[4, d], a_recv.at[4, d], here.at_seq(to))

    own_d = pltpu.make_async_copy(d_out.at[here.seq], dh_ref.at[rows(here.seq), :], own_sem.at[4])

    def quarter(x):
        return mine.at[:, pl.ds(pl.multiple_of(x * 4 * HEAD, 4 * HEAD), 4 * HEAD)]

    def att_x(d):
        x = (here.x + d) % NX
        return remote(quarter(x), att4.at[here.x], m_send.at[d], m_recv.at[d], here.at_x(x))

    own_att_x = pltpu.make_async_copy(quarter(here.x), att4.at[here.x], m_send.at[0])

    pairs = ((q_ref, qh_ref), (k_ref, kh_ref), (v_ref, vh_ref))
    order = [(0, SAME_Y), (1, SAME_Y), (0, OTHER_Y), (1, OTHER_Y), (2, SAME_Y), (2, OTHER_Y)]
    queue = Queue((moved, *pairs[a], a, d) for a, ds in order for d in ds)
    each(1, NZ, lambda d: along_z(d).start())
    queue.start(14)
    for a, (src, dst) in enumerate(pairs):
        kept(src, dst, a).start()
    each(1, NZ, lambda d: along_z(d).wait_recv())
    along_y(0, 0).start()
    along_y(1, 0).start()
    on(0)
    for k in range(3):
        for way in range(2):
            along_y(way, k).wait_recv()
            along_y(way, k + 1).start()
            on(1 + 2 * k + way)
            queue.start(3)
    along_y(0, 3).wait_recv()
    along_y(1, 3).wait_recv()
    on(7)

    def next_x(j):
        for way in range(2):
            along_x(way, j).wait_recv()
            if j % 2 == way:
                from_x(way, j).start()
            queue.start(2)
            to_core(3 if way == 0 else 1, j).start()

    for j in range(4):
        next_x(j)

    arrived(*pairs[0], 0)
    arrived(*pairs[1], 1)

    def softmax(step):
        blocks = [step * TOGETHER + i for i in range(TOGETHER)]
        logits = [dot(qh_ref[b], gathered(kh_ref, listed(ids_ref, b)), 1, 1) * SCALE for b in blocks]
        expo = [jnp.exp(x - jnp.max(x, axis=1, keepdims=True)) for x in logits]
        for b, x in zip(blocks, expo):
            probs_ref[b] = x / jnp.sum(x, axis=1, keepdims=True)

    steps = SEQ_LEN // BLOCK // TOGETHER // 4
    for j in range(4):
        each(j * steps, (j + 1) * steps, softmax)
        next_x(4 + j)
    arrived(*pairs[2], 2)

    def attend(chunks):
        blocks = [2 * c + i for c in chunks for i in range(2)]
        out = [dot(probs_ref[b].astype(BF16), gathered(vh_ref, listed(ids_ref, b)), 1, 0) for b in blocks]
        for b, x in zip(blocks, out):
            att_out[block(b), :] = x.astype(BF16)

    def attend_and_send(i):
        attend([seq_at(i + 1), seq_at(15 - i)])
        att(i + 1).start()
        att(15 - i).start()

    each(0, 7, attend_and_send)
    attend([seq_at(8), here.seq])
    att(8).start()
    own_att.start()
    for j in range(8):
        from_x(j % 2, j).wait_recv()
        to_core(2, j).start()
    own_grads.start()
    each(1, NX, lambda d: grads(d).start())
    for i in (0, 3, 1, 2):
        for j in range(8):
            to_core(i, j).wait_recv()

    def project(head):
        d_out[head] = jnp.dot(g_ref[...], w_all[head % 2, head // 2], preferred_element_type=F32).astype(BF16)

    def project_and_send(d):
        project(seq_at(d))
        d_att(d).start()

    def project_both_ways(i):
        project_and_send(i + 1)
        project_and_send(15 - i)

    each(0, 7, project_both_ways)
    project_and_send(8)
    project(here.seq)
    own_d.start()

    def returned(src, dst, a, d):
        to = seq_at(d)
        return remote(
            src.at[rows(to), :], dst.at[:, cols(here.seq)], b_send.at[a, d], b_recv.at[a, d], here.at_seq(to)
        )

    def retained(src, dst, a):
        return pltpu.make_async_copy(src.at[rows(here.seq), :], dst.at[:, cols(here.seq)], own_back.at[a])

    def cleared(step):
        k_sum[block(step), :] = jnp.zeros((BLOCK, HEAD), F32)
        v_sum[block(step), :] = jnp.zeros((BLOCK, HEAD), F32)

    each(0, SEQ_LEN // BLOCK, cleared)

    def add(total, place, terms):
        total[block(place), :] += terms

    def backward(chunks):
        blocks = [2 * c + i for c in chunks for i in range(2)]
        at = [listed(ids_ref, b) for b in blocks]
        d = [dh_ref[block(b), :] for b in blocks]
        probs = [probs_ref[b] for b in blocks]
        d_probs = [dot(x, gathered(vh_ref, i), 1, 1) for x, i in zip(d, at)]
        delta = [jnp.sum(x * y, axis=1, keepdims=True) for x, y in zip(probs, d_probs)]
        d_logits = [(x * (y - z) * SCALE).astype(BF16) for x, y, z in zip(probs, d_probs, delta)]
        dq = [dot(x, gathered(kh_ref, i), 1, 0) for x, i in zip(d_logits, at)]
        for b, x in zip(blocks, dq):
            q_out[block(b), :] = x.astype(BF16)
        dk = [dot(x, qh_ref[b], 0, 0) for x, b in zip(d_logits, blocks)]
        dv = [dot(x.astype(BF16), y, 0, 0) for x, y in zip(probs, d)]
        for total, drawn, terms in ((k_sum, k_drawn, dk), (v_sum, v_drawn, dv)):
            for b, x in zip(blocks, terms):
                for s in range(3):
                    add(total, fixed(b)[s], x[s * BLOCK : (s + 1) * BLOCK])
                for s in range(5, SLOTS):
                    drawn[block((s - 5) * 32 + b), :] = x[s * BLOCK : (s + 1) * BLOCK]
            for s in (3, 4):
                add(total, fixed(0)[s], sum(x[s * BLOCK : (s + 1) * BLOCK] for x in terms))

    def chunk_from(d):
        return (here.seq + 16 - d) % 16

    def backward_and_send(i):
        d_att(i + 1).wait_recv()
        d_att(15 - i).wait_recv()
        backward([chunk_from(i + 1), chunk_from(15 - i)])
        returned(q_out, dq_ref, 0, 15 - i).start()
        returned(q_out, dq_ref, 0, i + 1).start()

    own_att.wait()
    each(1, 16, lambda d: att(d).wait_recv())
    att_copy = pltpu.make_async_copy(mine, att_ref, own_sem.at[5])
    att_copy.start()
    own_att_x.start()
    each(1, NX, lambda d: att_x(d).start())
    own_d.wait()
    each(0, 7, backward_and_send)
    d_att(8).wait_recv()
    backward([chunk_from(8), here.seq])
    returned(q_out, dq_ref, 0, 8).start()
    retained(q_out, dq_ref, 0).start()

    drawn = drawn_ref[...]
    hits = (lax.broadcasted_iota(jnp.int32, (32, 96), 0) == jnp.broadcast_to(drawn, (32, 96))).astype(F32).astype(BF16)
    hits = jnp.concatenate([hits, hits], axis=1)

    def gather_terms(r):
        for total, terms in ((k_sum, k_drawn), (v_sum, v_drawn)):
            x = terms[pl.ds(r, 96, stride=BLOCK), :]
            high = x.astype(BF16)
            low = (x - high.astype(F32)).astype(BF16)
            mine_too = jnp.dot(hits, jnp.concatenate([high, low], axis=0), preferred_element_type=F32)
            at = pl.ds(r, 32, stride=BLOCK)
            total[at, :] = total[at, :] + mine_too

    def gather_some(i):
        for r in range(4):
            gather_terms(4 * i + r)

    each(0, BLOCK // 4, gather_some)
    k_out[...] = k_sum[...].astype(BF16)
    v_out[...] = v_sum[...].astype(BF16)
    order = [(1, SAME_Y), (2, SAME_Y), (1, OTHER_Y), (2, OTHER_Y)]
    results = ((q_out, dq_ref), (k_out, dk_ref), (v_out, dv_ref))
    back = Queue((returned, *results[a], a, d) for a, ds in order for d in ds)
    retained(k_out, dk_ref, 1).start()
    retained(v_out, dv_ref, 2).start()
    back.start(14)

    own_att_x.wait()
    own_grads.wait()
    each(1, NX, lambda d: att_x(d).wait_recv())
    each(1, NX, lambda d: grads(d).wait_recv())

    def multiply(i):
        head, y_hi = i // 4, i % 4
        a = att4[:, :, cols(head)].reshape(NX * ROWS, HEAD)
        g = g4[:, :, pl.ds(pl.multiple_of(y_hi * 4 * HEAD, 4 * HEAD), 4 * HEAD)].reshape(NX * ROWS, 4 * HEAD)
        total = dot(a, g, 0, 0)
        product[i] = total
        p_out[i] = total.astype(BF16)

    each(0, HEADS, multiply)

    def half_rows(core):
        return pl.ds(pl.multiple_of(core * 64, 64), 64)

    to_half = remote(
        p_out.at[:, half_rows(1 - here.core), :], p_in, p_send.at[0], p_recv.at[0], here.other_core()
    )
    to_half.start()

    to_half.wait()

    def add_core(i):
        head, y_hi = i // 4, i % 4
        total = product[i, half_rows(here.core), :] + p_in[i].astype(F32)
        for x in range(NX):
            slot = (1 - head // 2) * 4 + x
            y_out[2 * y_hi + head % 2, slot] = total[:, x * HEAD : (x + 1) * HEAD].astype(BF16)

    each(0, HEADS, add_core)

    def half_of(k, way):
        return slice(None) if k > 0 else pl.ds(4 * way, 4)

    def target(way, k):
        return (here.y + (4 - k if way == 0 else 4 + k)) % NY

    def sum_y(way, k):
        part = half_of(k, way)
        return remote(
            y_out.at[target(way, k), part], y_in.at[4 * way + k, part], s_send.at[way, k], s_recv.at[way, k],
            up if way == 0 else down,
        )

    def next_y(k):
        for way in range(2):
            sum_y(way, k - 1).wait_recv()
            low = 0 if k > 1 else 4 * way

            def add_y(slot):
                mine_too = y_out[target(way, k), slot].astype(F32)
                y_out[target(way, k), slot] = (mine_too + y_in[4 * way + k - 1, slot].astype(F32)).astype(BF16)

            each(low, NZ if k > 1 else low + 4, add_y)
            sum_y(way, k).start()

    sum_y(0, 0).start()
    sum_y(1, 0).start()

    next_y(1)
    back.start(5)
    next_y(2)
    back.start(5)
    next_y(3)
    back.start(6)
    sum_y(0, 3).wait_recv()
    sum_y(1, 3).wait_recv()

    def finish_y(z):
        total = y_out[here.y, z].astype(F32) + y_in[3, z].astype(F32) + y_in[7, z].astype(F32)
        z_out[z] = total.astype(BF16)

    each(0, NZ, finish_y)

    def sum_z(d):
        z = (here.z + d) % NZ
        return remote(z_out.at[z], z_in.at[d], t_send.at[d], t_recv.at[d], here.at_z(z))

    each(1, NZ, lambda d: sum_z(d).start())
    each(1, NZ, lambda d: sum_z(d).wait())
    total = z_out[here.z].astype(F32)
    for d in range(1, NZ):
        total += z_in[d].astype(F32)
    last_out[...] = total

    def to_owner(core):
        to = (here.dp_of(x=here.z % 4, core=core), 2 * (2 * here.x + 1 - here.z // 4) + here.y_lo)
        return remote(last_out, last_in.at[here.core], n_send.at[core], n_recv.at[here.core], to)

    def from_owner(core):
        to = (here.dp_of(x=here.z % 4, core=core), 2 * (2 * here.x + 1 - here.z // 4) + here.y_lo)
        return remote(last_out, last_in.at[core], n_send.at[core], n_recv.at[core], to)

    for core in range(2):
        to_owner(core).start()
    for core in range(2):
        from_owner(core).wait_recv()
    first = here.core == 0
    top, bottom = last_in[0], last_in[1]
    gw_ref[:64, :] = jnp.where(first, top[:, :64], top[:, 64:])
    gw_ref[64:, :] = jnp.where(first, bottom[:, :64], bottom[:, 64:])

    for a, (src, dst) in enumerate(results):
        retained(src, dst, a).wait()
        each(1, 16, lambda d: returned(src, dst, a, d).wait())

    for a, (src, dst) in enumerate(pairs):
        each(1, 16, lambda d: moved(src, dst, a, d).wait_send())
    each(1, 16, lambda d: att(d).wait_send())
    each(1, 16, lambda d: d_att(d).wait_send())
    att_copy.wait()
    each(1, NX, lambda d: grads(d).wait_send())
    each(1, NX, lambda d: att_x(d).wait_send())
    for core in range(2):
        to_owner(core).wait_send()
    for way in range(2):
        for k in range(4):
            sum_y(way, k).wait_send()
    each(1, NZ, lambda d: along_z(d).wait_send())
    for way in range(2):
        for k in range(4):
            along_y(way, k).wait_send()
        for j in range(8):
            along_x(way, j).wait_send()
    for j in range(8):
        from_x(j % 2, j).wait_send()
        for i in range(4):
            to_core(i, j).wait_send()


def layer(ids, drawn, q, k, v, g, w):
    any_ = pl.BlockSpec(memory_space=pl.ANY)
    dma = pltpu.SemaphoreType.DMA
    flat = jax.ShapeDtypeStruct((ROWS, WIDTH), BF16)
    by_head, by_block = (SEQ_LEN, HEAD), (SEQ_LEN // BLOCK, BLOCK, HEAD)
    return pl.pallas_call(
        layer_kernel,
        out_shape=(flat,) * 4 + (jax.ShapeDtypeStruct((HEAD, 64), F32),),
        in_specs=[pl.BlockSpec(memory_space=pltpu.SMEM), VMEM] + [pl.BlockSpec(memory_space=pltpu.HBM)] * 3 + [VMEM] * 2,
        out_specs=(any_,) * 4 + (VMEM,),
        scratch_shapes=[
            pltpu.VMEM(by_block, BF16),
            pltpu.VMEM(by_block, BF16),
            pltpu.VMEM(by_block, BF16),
            pltpu.VMEM(by_head, BF16),
            pltpu.VMEM((SEQ_LEN // BLOCK, BLOCK, SLOTS * BLOCK), F32),
            pltpu.VMEM((ROWS, WIDTH), BF16),
            pltpu.VMEM((NX, ROWS, 4 * HEAD), BF16),
            pltpu.VMEM((NX, ROWS, WIDTH), BF16),
            pltpu.VMEM((2, NZ, WIDTH, HEAD), BF16),
            pltpu.VMEM(by_head, BF16),
            pltpu.VMEM((HEADS, ROWS, HEAD), BF16),
            pltpu.VMEM(by_head, BF16),
            pltpu.VMEM(by_head, BF16),
            pltpu.VMEM(by_head, BF16),
            pltpu.VMEM(by_head, F32),
            pltpu.VMEM(by_head, F32),
            pltpu.VMEM((96 * BLOCK, HEAD), F32),
            pltpu.VMEM((96 * BLOCK, HEAD), F32),
            pltpu.VMEM((HEADS, HEAD, 4 * HEAD), F32),
            pltpu.VMEM((HEADS, HEAD, 4 * HEAD), BF16),
            pltpu.VMEM((HEADS, 64, 4 * HEAD), BF16),
            pltpu.VMEM((NY, NZ, 64, HEAD), BF16),
            pltpu.VMEM((NY, NZ, 64, HEAD), BF16),
            pltpu.VMEM((NZ, 64, HEAD), BF16),
            pltpu.VMEM((NZ, 64, HEAD), BF16),
            pltpu.VMEM((64, HEAD), F32),
            pltpu.VMEM((2, 64, HEAD), F32),
            dma((5, 16)), dma((5, 16)), dma((6,)), dma((NZ,)), dma((NZ,)), dma((2, 4)), dma((2, 4)),
            dma((2, 8)), dma((2, 8)), dma((8,)), dma((8,)), dma((4, 8)), dma((4, 8)),
            dma((4,)), dma((4,)), dma((4,)), dma((4,)), dma((2,)), dma((2,)),
            dma((3, 16)), dma((3, 16)), dma((3,)), dma((1,)), dma((1,)),
            dma((2, 4)), dma((2, 4)), dma((NZ,)), dma((NZ,)),
        ],
        compiler_params=pltpu.CompilerParams(
            collective_id=0, has_side_effects=True, vmem_limit_bytes=50 * 2**20
        ),
        name="layer",
    )(ids, drawn, q, k, v, g, w)


def in_blocks(flat):
    return flat.reshape(ROWS // BLOCK, BLOCK, WIDTH)


def local(query_rows, key_rows, value_rows, out_weight, grad_out, block_list):
    ids = block_list[0]
    drawn = ids[:, 5:].T.reshape(1, 96)
    att, dq, dk, dv, grad_weight = layer(
        ids, drawn, in_blocks(query_rows), in_blocks(key_rows), in_blocks(value_rows), grad_out[0], out_weight
    )
    return (att[None], dq[None], dk[None], dv[None], grad_weight)


def solution(mesh):
    return jax.shard_map(
        local,
        mesh=mesh,
        in_specs=(
            P("dp", "seq", None),
            P("dp", "seq", None),
            P("dp", "seq", None),
            P("seq", "dp"),
            P("dp", "seq", None),
            P("dp", None, None),
        ),
        out_specs=(
            P("dp", "seq", None),
            P("dp", "seq", None),
            P("dp", "seq", None),
            P("dp", "seq", None),
            P("seq", "dp"),
        ),
        check_vma=False,
    )
```
